256 devices in a mesh: resp: 32 (over z, y_hi, core), head: 8 (over y_lo, x).
Axes of the slice: x: 4, y: 4 (y_hi: 2, y_lo: 2; y = y_hi * 2 + y_lo), z: 8, core: 2. Of those that a mesh axis runs over, the one named last changes fastest.
Arguments:
- queries: bfloat16 [8192, 4096], P('resp', 'head'), may hold values from -512 to 512
- resp_keys: bfloat16 [8192, 1024], P('resp', 'head'), may hold values from -6 to 6
- resp_values: bfloat16 [8192, 1024], P('resp', 'head'), may hold values from -6 to 6
- prompt_keys: bfloat16 [16384, 1024], P('resp', 'head'), may hold values from -6 to 6
- prompt_values: bfloat16 [16384, 1024], P('resp', 'head'), may hold values from -6 to 6
- lengths: int32 [128], P('resp'), may hold values from 1 to 64, as said below
- out_weight: bfloat16 [4096, 8192], P('head'), may hold values from -0.5 to 0.5
Outputs:
- mixed: bfloat16 [8192, 8192], P('resp', 'head')
The draws below stay inside these ranges and needn't reach their ends.
Inputs may be any that keep to these rules, and one draw needn't show every extreme that they name: `lengths`: every response has between 1 and 64 live tokens, and some response has all 64.
All inputs are finite; a program needn't handle non-finite values.
Results may differ from the reference program's by a relative error of at most 0.02.
Values may be sent and summed in bfloat16 or wider, within the bound.
No kernel may reach another device: no remote copies, remote signals or barrier semaphores. Data moves between devices by JAX's collectives and lax.ppermute only.
A program may use at most 64 MiB of HBM per device.

```python
import math
import jax
import jax.numpy as jnp
from jax import lax

D = 8192
HD = 128
KVH = 8
GROUP = 4
QH = 32
RESP_LEN = 64
RESPONSES = 128
ROWS = 8192
PROMPT = 16384


def draw_prompt_keys(key, part):
    key = jax.random.fold_in(key, 11)
    result = jnp.clip(jax.random.normal(key, (PROMPT, KVH * HD), jnp.float32), -6.0, 6.0)
    return result.astype(jnp.bfloat16)


def draw_queries(key, part):
    key = jax.random.fold_in(key, 12)
    result = 2.5 * jnp.clip(jax.random.normal(key, (ROWS, QH * HD), jnp.float32), -6.0, 6.0)
    return result.astype(jnp.bfloat16)


def draw_lengths(key, part):
    key = jax.random.fold_in(key, 13)
    drawn = jax.random.randint(key, (RESPONSES,), 1, RESP_LEN + 1)
    chosen_slot = jax.random.randint(jax.random.fold_in(key, 1), (), 0, RESPONSES)
    return drawn.at[chosen_slot].set(RESP_LEN).astype(jnp.int32)


def raised(values, own_key, source, target, blocks, factor):
    owner, partner = [(jnp.arange(values.shape[position]) // (values.shape[position] // blocks)).reshape([-1 if axis == position else 1 for axis in range(values.ndim)]) for position in (source, target)]
    chosen = jax.random.permutation(own_key, blocks)[partner]
    strong = (owner == chosen) | (owner == (partner + blocks // 2) % blocks)
    return jnp.where(strong, factor * values, values)


def shard_levels(own_key, extent, pieces, low, top_value):
    loudness, own = 1.0, jax.random.fold_in(own_key, 6)
    for axis_at, blocks in pieces:
        heights = jnp.exp(jax.random.uniform(jax.random.fold_in(own, axis_at), (blocks,), jnp.float32, low / len(pieces), top_value / len(pieces)))
        loudness = loudness * jnp.repeat(heights, extent[axis_at] // blocks).reshape([-1 if axis == axis_at else 1 for axis in range(len(extent))])
    return loudness


def bell_draw(key, shape, scale, bound, split=(), held_as=jnp.bfloat16):
    values = scale * jax.random.normal(key, shape, jnp.float32)
    if split:
        values = values * shard_levels(key, shape, split, -0.22, 0.18)
    return jnp.clip(values, -bound, bound).astype(held_as)


def bell_draw_with(key, shape, deviation, limit, shards, heavy, kind=jnp.bfloat16):
    values = deviation * jax.random.normal(key, shape, jnp.float32)
    if shards:
        values = values * shard_levels(key, shape, shards, -0.22, 0.18)
    return jnp.clip(raised(values, jax.random.fold_in(key, 3), *heavy), -limit, limit).astype(kind)


def setup_inputs(seed: int = 0) -> dict:
    streams_of = jax.random.split(jax.random.key(seed), 8)
    return {
        "queries": draw_queries(jax.random.fold_in(streams_of[7], 71), 0),
        "resp_keys": bell_draw(streams_of[1], (ROWS, KVH * HD), 1.0, 6.0, ((0, 32), (1, 8))),
        "resp_values": bell_draw(streams_of[2], (ROWS, KVH * HD), 1.0, 6.0, ((0, 32), (1, 8))),
        "prompt_keys": draw_prompt_keys(jax.random.fold_in(streams_of[7], 71), 0),
        "prompt_values": bell_draw(streams_of[4], (PROMPT, KVH * HD), 1.0, 6.0, ((0, 32), (1, 8))),
        "lengths": draw_lengths(jax.random.fold_in(streams_of[7], 71), 0),
        "out_weight": bell_draw_with(streams_of[6], (QH * HD, D), (QH * HD // 16) ** -0.5, 0.5, ((0, 8),), (0, 1, 8, 2.0)),
    }


def reference(queries, resp_keys, resp_values, prompt_keys, prompt_values, lengths, out_weight):
    scale = HD ** -0.5
    block = math.gcd(RESPONSES, 8)
    count = RESPONSES // block
    slots = jnp.arange(RESP_LEN, dtype=jnp.int32)
    causal = slots[None, :] <= slots[:, None]

    def one_head(head_index):
        q_all = lax.dynamic_slice_in_dim(queries, (head_index * GROUP * HD).astype(jnp.int32), GROUP * HD, 1)
        q_all = q_all.reshape(count, block, RESP_LEN, GROUP, HD)
        key_cache = lax.dynamic_slice_in_dim(prompt_keys, (head_index * HD).astype(jnp.int32), HD, 1).astype(jnp.float32)
        value_cache = lax.dynamic_slice_in_dim(prompt_values, (head_index * HD).astype(jnp.int32), HD, 1).astype(jnp.float32)
        own_keys = lax.dynamic_slice_in_dim(resp_keys, (head_index * HD).astype(jnp.int32), HD, 1).reshape(count, block, RESP_LEN, HD)
        own_values = lax.dynamic_slice_in_dim(resp_values, (head_index * HD).astype(jnp.int32), HD, 1).reshape(count, block, RESP_LEN, HD)
        lens = lengths.reshape(count, block)

        def one_block(items):
            query, keys_self, values_self, live = items
            query = query.astype(jnp.float32)
            prompt_score = jnp.einsum('rqgd,kd->rqgk', query, key_cache) * scale
            self_score = jnp.einsum('rqgd,rkd->rqgk', query, keys_self.astype(jnp.float32)) * scale
            keep = causal[None, :, None, :] & (slots[None, None, None, :] < live[:, None, None, None])
            self_score = jnp.where(keep, self_score, jnp.float32(-1e30))
            top = jnp.maximum(jnp.max(prompt_score, -1), jnp.max(self_score, -1))
            weight_prompt = jnp.exp(prompt_score - top[..., None])
            weight_self = jnp.exp(self_score - top[..., None])
            total = jnp.sum(weight_prompt, -1) + jnp.sum(weight_self, -1)
            wp_round = weight_prompt.astype(jnp.bfloat16).astype(jnp.float32)
            ws_round = weight_self.astype(jnp.bfloat16).astype(jnp.float32)
            numer = jnp.einsum('rqgk,kd->rqgd', wp_round, value_cache)
            numer = numer + jnp.einsum('rqgk,rkd->rqgd', ws_round, values_self.astype(jnp.float32))
            result = numer / total[..., None]
            alive = slots[None, :] < live[:, None]
            result = jnp.where(alive[:, :, None, None], result, jnp.float32(0.0))
            return result.astype(jnp.bfloat16)

        return lax.map(one_block, (q_all, own_keys, own_values, lens))

    heads_out = lax.map(one_head, jnp.arange(KVH, dtype=jnp.int32))
    heads_out = heads_out.reshape(KVH, RESPONSES, RESP_LEN, GROUP, HD)
    attended = jnp.transpose(heads_out, (1, 2, 0, 3, 4)).reshape(ROWS, QH * HD)

    def add_group(index, acc):
        start = (index * GROUP * HD).astype(jnp.int32)
        cols = lax.dynamic_slice_in_dim(attended, start, GROUP * HD, 1)
        rows = lax.dynamic_slice_in_dim(out_weight, start, GROUP * HD, 0)
        partial_value = jnp.dot(cols, rows, preferred_element_type=jnp.float32).astype(jnp.bfloat16)
        partial_value = lax.optimization_barrier(partial_value)
        return acc + partial_value.astype(jnp.float32)

    summed = lax.fori_loop(jnp.int32(0), jnp.int32(KVH), add_group, jnp.zeros((ROWS, D), jnp.float32))
    return summed.astype(jnp.bfloat16)
```

```python
import functools
import math

import jax
import jax.numpy as jnp
from jax import lax
from jax.experimental import pallas as pl
from jax.experimental.pallas import tpu as pltpu
from jax.sharding import Mesh, PartitionSpec as P

NEG = -1e30
TILE = 256
NT = (((1,), (1,)), ((), ()))


def ring(size, step):
    return [(i, (i + step) % size) for i in range(size)]


def opposite(size, step):
    pairs = []
    for place in range(size):
        pairs.append((2 * place, 2 * ((place + step) % size)))
        pairs.append((2 * place + 1, 2 * ((place - step) % size) + 1))
    return pairs


def opposite_x(size, step):
    forward = [(i, (i + step) % size) for i in range(size)]
    backward = [(size + i, size + (i - step) % size) for i in range(size)]
    return forward + backward


def fold(tiles, scale, query, blocks, read, write, extra=None):
    keys = [ref[:, :128] for ref in blocks]
    values = [
        jnp.concatenate([ref[:, 128:], jnp.ones((ref.shape[0], 128), jnp.bfloat16)], 1)
        for ref in blocks
    ]

    def score(tile):
        parts = [
            lax.dot_general(query(tile), key, NT, preferred_element_type=jnp.float32)
            for key in keys
        ]
        return parts

    def finish(item):
        tile, weights, shrink, top, old = item
        total = None
        for weight, value in zip(weights, values + ([extra[1]] if extra else [])):
            term = jnp.dot(weight, value, preferred_element_type=jnp.float32)
            total = term if total is None else total + term
        accum, count = total[:, :128], total[:, 128:]
        if old is not None:
            accum = accum + old[0] * shrink
            count = count + old[1] * shrink
        write(tile, accum, top, count)

    upcoming = score(tiles[0])
    waiting = None
    for place, tile in enumerate(tiles):
        scores = [part * scale for part in upcoming]
        if place + 1 < len(tiles):
            upcoming = score(tiles[place + 1])
        if waiting is not None:
            finish(waiting)
        if extra is not None:
            scores = scores + [extra[0](tile)]
        old = read(tile)
        top = functools.reduce(jnp.maximum, [jnp.max(part, 1, keepdims=True) for part in scores])
        shrink = None
        if old is not None:
            top = jnp.maximum(top, old[2])
            shrink = jnp.exp2(old[2] - top)
        weights = [jnp.exp2(part - top).astype(jnp.bfloat16) for part in scores]
        waiting = (tile, weights, shrink, top, old)
    finish(waiting)


def pack(top, count):
    lane = lax.broadcasted_iota(jnp.int32, count.shape, 1)
    return jnp.where(lane < 64, jnp.broadcast_to(top, count.shape), count)


def first_kernel(scale, group, resp_len, lengths, q_ref, kv_ref, self_ref, acc_ref, ml_ref):
    own = pl.program_id(0) == 0
    rows = q_ref.shape[0]
    shape = (rows, rows)
    slot = lax.broadcasted_iota(jnp.int32, shape, 0)
    other = lax.broadcasted_iota(jnp.int32, shape, 1)
    live = jnp.zeros(shape, jnp.int32)
    for index in range(rows // resp_len):
        live = jnp.where(other // resp_len == index, lengths[index], live)
    keep = (slot // resp_len == other // resp_len) & (other <= slot)
    keep = keep & (other % resp_len < live) & own
    own_keys = self_ref[:, :128]
    own_values = jnp.concatenate([self_ref[:, 128:], jnp.ones((rows, 128), jnp.bfloat16)], 1)

    def query(tile):
        return q_ref[:, tile * 128 : (tile + 1) * 128]

    def self_scores(tile):
        scores = lax.dot_general(query(tile), own_keys, NT, preferred_element_type=jnp.float32)
        return jnp.where(keep, scores * scale, NEG)

    def write(tile, accum, top, count):
        at = pl.ds(tile * rows, rows)
        acc_ref[at, :] = accum
        ml_ref[at, :] = pack(top, count)

    fold(
        list(range(group)), scale, query, [kv_ref], lambda tile: None, write,
        (self_scores, own_values),
    )


def next_kernel(scale, group, count_kv, q_ref, *refs):
    kv_refs = refs[:count_kv]
    acc_in, ml_in, acc_ref, ml_ref = refs[count_kv:]
    rows = q_ref.shape[0]

    def query(tile):
        return q_ref[:, tile * 128 : (tile + 1) * 128]

    def read(tile):
        at = pl.ds(tile * rows, rows)
        packed = ml_in[at, :]
        return acc_in[at, :], packed[:, 64:65], packed[:, :1]

    def write(tile, accum, top, count):
        at = pl.ds(tile * rows, rows)
        acc_ref[at, :] = accum
        ml_ref[at, :] = pack(top, count)

    fold(list(range(group)), scale, query, list(kv_refs), read, write)


def params():
    return pltpu.CompilerParams(vmem_limit_bytes=44 * 2**20)


def cost(rows, keys, extra):
    return pl.CostEstimate(
        flops=4 * rows * keys * 128, bytes_accessed=extra, transcendentals=rows * keys
    )


def first_call(scale, group, resp_len, lengths, q, kv, self_kv):
    slots = 256
    sets = q.shape[0] // slots
    rows = slots * group
    state = jax.ShapeDtypeStruct((sets * rows, 128), jnp.float32)
    block = pl.BlockSpec((rows, 128), lambda i, *_: (i, 0))
    whole = lambda x: pl.BlockSpec(x.shape, lambda i, *_: (0, 0))
    return pl.pallas_call(
        functools.partial(first_kernel, scale, group, resp_len),
        grid_spec=pltpu.PrefetchScalarGridSpec(
            num_scalar_prefetch=1,
            grid=(sets,),
            in_specs=[
                pl.BlockSpec((slots, group * 128), lambda i, *_: (i, 0)),
                whole(kv),
                whole(self_kv),
            ],
            out_specs=[block, block],
        ),
        out_shape=[state, state],
        compiler_params=params(),
        cost_estimate=cost(sets * rows, kv.shape[0] + slots, 3 * 2**20),
        name="attend_first",
    )(lengths, q, kv, self_kv)


def next_call(scale, group, q, kvs, acc, ml):
    slots = 256
    sets = q.shape[0] // slots
    rows = slots * group
    state = jax.ShapeDtypeStruct(acc.shape, jnp.float32)
    block = pl.BlockSpec((rows, 128), lambda i: (i, 0))
    whole = lambda x: pl.BlockSpec(x.shape, lambda i: (0, 0))
    keys = sum(kv.shape[0] for kv in kvs)
    return pl.pallas_call(
        functools.partial(next_kernel, scale, group, len(kvs)),
        grid=(sets,),
        in_specs=[pl.BlockSpec((slots, group * 128), lambda i: (i, 0))]
        + [whole(kv) for kv in kvs]
        + [block, block],
        out_specs=[block, block],
        out_shape=[state, state],
        compiler_params=params(),
        cost_estimate=cost(sets * rows, keys, 5 * 2**20),
        name="attend_next",
    )(q, *kvs, acc, ml)


def merge_kernel(group, resp_len, lengths, acc_a, ml_a, acc_b, ml_b, out_ref):
    rows = out_ref.shape[0]
    slot = lax.broadcasted_iota(jnp.int32, (rows, 128), 0)
    live = jnp.zeros((rows, 128), jnp.int32)
    for index in range(rows // resp_len):
        live = jnp.where(slot // resp_len == index, lengths[index], live)
    alive = slot % resp_len < live
    for head in range(group):
        at = pl.ds(head * rows, rows)
        first, second = ml_a[at, :], ml_b[at, :]
        top_a, top_b = first[:, :1], second[:, :1]
        top = jnp.maximum(top_a, top_b)
        scale_a, scale_b = jnp.exp2(top_a - top), jnp.exp2(top_b - top)
        total = first[:, 64:65] * scale_a + second[:, 64:65] * scale_b
        accum = acc_a[at, :] * scale_a + acc_b[at, :] * scale_b
        result = jnp.where(alive, accum / total, 0.0)
        out_ref[:, head * 128 : (head + 1) * 128] = result.astype(jnp.bfloat16)


def merge_call(group, resp_len, lengths, acc, ml, acc_b, ml_b):
    rows = acc_b.shape[0]
    slots = rows // group
    block = pl.BlockSpec((rows, 128), lambda i, *_: (0, 0))
    return pl.pallas_call(
        functools.partial(merge_kernel, group, resp_len),
        grid_spec=pltpu.PrefetchScalarGridSpec(
            num_scalar_prefetch=1,
            grid=(1,),
            in_specs=[block] * 4,
            out_specs=pl.BlockSpec((slots, group * 128), lambda i, *_: (0, 0)),
        ),
        out_shape=jax.ShapeDtypeStruct((slots, group * 128), jnp.bfloat16),
        compiler_params=params(),
        name="merge",
    )(lengths, acc, ml, acc_b, ml_b)


def per_device(queries, resp_keys, resp_values, prompt_keys, prompt_values, lengths, out_weight):
    head_size = prompt_keys.shape[1]
    slots = queries.shape[0]
    group = queries.shape[1] // head_size
    resp_len = slots // lengths.shape[0]
    scale = head_size ** (-0.5) * math.log2(math.e)
    z_size = lax.axis_size("z")
    x_size = lax.axis_size("x")
    core = lax.axis_index("core")
    x_at = lax.axis_index("x")
    yl_at = lax.axis_index("yl")

    swap_core = lambda v: lax.ppermute(v, "core", ring(2, 1))
    swap_yh = lambda v: lax.ppermute(v, "yh", ring(2, 1))
    swap_yl = lambda v: lax.ppermute(v, "yl", ring(2, 1))
    z_hop = lambda v: lax.ppermute(v, ("z", "core"), opposite(z_size, 1))
    x_hop = lambda v: lax.ppermute(v, ("core", "x"), opposite_x(x_size, 1))
    x_back = lambda v: lax.ppermute(v, ("core", "x"), opposite_x(x_size, -1))
    x_far = lambda v: lax.ppermute(v, "x", ring(x_size, 2))

    after = lax.optimization_barrier

    kv = jnp.concatenate([prompt_keys, prompt_values], 1)
    self_kv = jnp.concatenate([resp_keys, resp_values], 1)
    half = kv.shape[0]
    kv_core = swap_core(kv)
    q_core = swap_core(queries)
    kv_y = swap_yh(kv)
    pair, q_core = after((jnp.concatenate([kv, kv_core], 0), q_core))
    a_1 = z_hop(pair)

    share = out_weight.shape[1] // (x_size * 2)
    part = share // 2

    def columns(x_to):
        mine = ((yl_at * x_size + x_to) * 2 + core) * part
        other = (((1 - yl_at) * x_size + x_to) * 2 + core) * part
        return jnp.concatenate(
            [lax.dynamic_slice_in_dim(out_weight, at, part, 1) for at in (mine, other)], 1
        )

    forward = jnp.where(core == 0, 1, x_size - 1)
    w_near = columns((x_at + forward) % x_size)
    w_back = columns((x_at + x_size - forward) % x_size)
    w_far = columns((x_at + 2) % x_size)
    q = jnp.concatenate([queries, q_core], 0)
    q, w_near, w_back, w_far = after((q, w_near, w_back, w_far))
    w_near, w_back, w_far = x_hop(w_near), x_back(w_back), x_far(w_far)

    acc, ml = first_call(scale, group, resp_len, lengths, q, kv, self_kv)
    acc, a_1, kv_y = after((acc, a_1, kv_y))
    a_2 = z_hop(a_1)
    b_1 = z_hop(jnp.concatenate([kv_y, swap_core(kv_y)], 0))
    acc, ml = next_call(scale, group, q, [kv_y, a_1], acc, ml)
    acc, a_2, b_1 = after((acc, a_2, b_1))
    a_3 = z_hop(a_2)
    b_2 = z_hop(b_1)
    acc, ml = next_call(scale, group, q, [a_2, b_1], acc, ml)
    acc, a_3, b_2 = after((acc, a_3, b_2))
    a_4 = z_hop(a_3[:half])
    b_3 = z_hop(b_2)
    acc, ml = next_call(scale, group, q, [a_3, b_2], acc, ml)
    acc, a_4, b_3, w_near, w_back, w_far = after((acc, a_4, b_3, w_near, w_back, w_far))
    b_4 = z_hop(b_3[:half])
    acc, ml = next_call(scale, group, q, [a_4, b_3], acc, ml)
    acc, ml = next_call(scale, group, q, [b_4], acc, ml)
    rows = slots * group
    attended = merge_call(
        group, resp_len, lengths, acc, ml, swap_core(acc[rows:]), swap_core(ml[rows:])
    )
    w_own = columns(x_at)

    both = jnp.concatenate([attended, swap_core(attended)], 0)
    near = x_hop(both)
    far = x_hop(near[:slots])
    back = swap_core(near)
    back = jnp.concatenate([back[slots:], back[:slots]], 0)
    far = jnp.concatenate([far, swap_core(far)], 0)
    partial = jnp.dot(
        jnp.concatenate([both, near, back, far], 1),
        jnp.concatenate([w_own, w_near, w_back, w_far], 0),
        preferred_element_type=jnp.float32,
    ).astype(jnp.bfloat16)
    summed = partial[:, :part].astype(jnp.float32) + swap_yl(partial[:, part:]).astype(jnp.float32)
    summed = summed.astype(jnp.bfloat16)
    mine, other = summed[:slots], swap_core(summed[slots:])
    low = jnp.where(core == 0, mine, other)
    high = jnp.where(core == 0, other, mine)
    return jnp.concatenate([low, high], 1)


def solution(mesh):
    fine = Mesh(mesh.devices.reshape(8, 2, 2, 2, 4), ("z", "yh", "core", "yl", "x"))
    resp, head = ("z", "yh", "core"), ("yl", "x")
    return jax.shard_map(
        per_device,
        mesh=fine,
        in_specs=(P(resp, head),) * 5 + (P(resp), P(head, None)),
        out_specs=P(resp, head),
        check_vma=False,
    )
```

```python
import functools
import math

import jax
import jax.numpy as jnp
from jax import lax
from jax.experimental import pallas as pl
from jax.experimental.pallas import tpu as pltpu
from jax.sharding import Mesh, PartitionSpec as P

NEG = -1e30
NT = (((1,), (1,)), ((), ()))


def ring(size, step):
    return [(i, (i + step) % size) for i in range(size)]


def opposite(size, step):
    pairs = []
    for place in range(size):
        pairs.append((2 * place, 2 * ((place + step) % size)))
        pairs.append((2 * place + 1, 2 * ((place - step) % size) + 1))
    return pairs


def opposite_x(size, step):
    forward = [(i, (i + step) % size) for i in range(size)]
    backward = [(size + i, size + (i - step) % size) for i in range(size)]
    return forward + backward


def lanes(x, width):
    return x if width == x.shape[1] else jnp.concatenate([x] * (width // x.shape[1]), 1)


def with_ones(values):
    return jnp.concatenate([values, jnp.ones((values.shape[0], 128), jnp.bfloat16)], 1)


def fold(tiles, scale, query, blocks, read, write, extra=None):
    keys = [block[:, :128] for block in blocks]
    values = [with_ones(block[:, 128:]) for block in blocks]

    def score(tile):
        return [
            lax.dot_general(query(tile), key, NT, preferred_element_type=jnp.float32)
            for key in keys
        ]

    def finish(item):
        tile, pairs, shrink, top, old = item
        total = None
        for weight, value in pairs:
            term = jnp.dot(weight, value, preferred_element_type=jnp.float32)
            total = term if total is None else total + term
        accum, count = total[:, :128], total[:, 128:]
        if old is not None:
            accum = accum + old[0] * shrink
            count = count + old[2] * shrink
        write(tile, accum, top, count)

    upcoming = score(tiles[0])
    waiting = None
    for place, tile in enumerate(tiles):
        scores, sides = upcoming, values
        if place + 1 < len(tiles):
            upcoming = score(tiles[place + 1])
        if waiting is not None:
            finish(waiting)
        own = extra(tile) if extra is not None else None
        if own is not None:
            scores, sides = scores + [own[0]], sides + [own[1]]
        peak = None
        for part in scores:
            for at in range(0, part.shape[1], 128):
                column = part[:, at : at + 128]
                peak = column if peak is None else jnp.maximum(peak, column)
        top = jnp.broadcast_to(jnp.max(peak, 1, keepdims=True), peak.shape) * scale
        old = read(tile)
        shrink = None
        if old is not None:
            top = jnp.maximum(top, old[1])
            shrink = jnp.exp2(old[1] - top)
        weights = [
            jnp.exp2(part * scale - lanes(top, part.shape[1])).astype(jnp.bfloat16)
            for part in scores
        ]
        waiting = (tile, list(zip(weights, sides)), shrink, top, old)
    finish(waiting)


def live_of(lengths, index, resp_len, count):
    live = jnp.zeros(index.shape, jnp.int32)
    for response in range(count):
        live = jnp.where(index // resp_len == response, lengths[response], live)
    return live


def attend_kernel(scale, group, resp_len, sets, rows_of, first, *refs):
    refs = list(refs)
    lengths, self_ref = (refs.pop(0), refs.pop(0)) if first else (None, None)
    queries = [refs.pop(0) for _ in range(sets)]
    blocks = [refs.pop(0)[:rows, :] for rows in rows_of]
    old = None if first else [[refs.pop(0) for _ in range(3)] for _ in range(sets)]
    new = [[refs.pop(0) for _ in range(3)] for _ in range(sets)]
    slots = queries[0].shape[0]
    tiles = [(index, head) for index in range(sets) for head in range(group)]

    def at(tile):
        return pl.ds(tile[1] * slots, slots)

    def query(tile):
        return queries[tile[0]][:, tile[1] * 128 : (tile[1] + 1) * 128]

    def read(tile):
        return None if first else [ref[at(tile), :] for ref in old[tile[0]]]

    def write(tile, *state):
        for ref, value in zip(new[tile[0]], state):
            ref[at(tile), :] = value

    extra = None
    if first:
        shape = (slots, slots)
        slot = lax.broadcasted_iota(jnp.int32, shape, 0)
        other = lax.broadcasted_iota(jnp.int32, shape, 1)
        keep = (slot // resp_len == other // resp_len) & (other <= slot)
        keep = keep & (other % resp_len < live_of(lengths, other, resp_len, slots // resp_len))
        own_values = with_ones(self_ref[:, 128:])

        def extra(tile):
            if tile[0] > 0:
                return None
            scores = lax.dot_general(
                query(tile), self_ref[:, :128], NT, preferred_element_type=jnp.float32
            )
            return jnp.where(keep, scores, NEG), own_values

    fold(tiles, scale, query, blocks, read, write, extra)


VMEM = pl.BlockSpec(memory_space=pltpu.VMEM)
SMEM = pl.BlockSpec(memory_space=pltpu.SMEM)


def params():
    return pltpu.CompilerParams(vmem_limit_bytes=32 * 2**20)


def attend(scale, group, resp_len, queries, blocks, states, first=None):
    sets, slots = len(queries), queries[0].shape[0]
    rows = slots * group
    head = list(first) if first else []
    operands = head + list(queries) + [block for block, _ in blocks]
    keys = sum(count for _, count in blocks)
    state = jax.ShapeDtypeStruct((rows, 128), jnp.float32)
    aliases = {}
    if not first:
        aliases = {len(operands) + i: i for i in range(3 * sets)}
        operands += [array for one in states for array in one]
    specs = [VMEM] * len(operands)
    if first:
        specs[0] = SMEM
    out = pl.pallas_call(
        functools.partial(
            attend_kernel, scale, group, resp_len, sets, [count for _, count in blocks], bool(first)
        ),
        in_specs=specs,
        out_specs=[VMEM] * (3 * sets),
        out_shape=[state] * (3 * sets),
        input_output_aliases=aliases,
        compiler_params=params(),
        cost_estimate=pl.CostEstimate(
            flops=16 * sets * rows * keys * 128, bytes_accessed=2**20, transcendentals=0
        ),
        name="attend",
    )(*operands)
    return [out[3 * i : 3 * i + 3] for i in range(sets)]


def ship_kernel(group, acc, top, total, out, stats):
    slots = out.shape[0]
    lane = lax.broadcasted_iota(jnp.int32, (slots, 128), 1) // 16
    packed = jnp.zeros((slots, 128), jnp.float32)
    for head in range(group):
        at = pl.ds(head * slots, slots)
        out[:, head * 128 : (head + 1) * 128] = (acc[at, :] / total[at, :]).astype(jnp.bfloat16)
        packed = jnp.where(lane == head, top[at, :], packed)
        packed = jnp.where(lane == group + head, total[at, :], packed)
    stats[...] = packed


def ship(group, state):
    slots = state[0].shape[0] // group
    return pl.pallas_call(
        functools.partial(ship_kernel, group),
        in_specs=[VMEM] * 3,
        out_specs=[VMEM] * 2,
        out_shape=[
            jax.ShapeDtypeStruct((slots, group * 128), jnp.bfloat16),
            jax.ShapeDtypeStruct((slots, 128), jnp.float32),
        ],
        compiler_params=params(),
        name="ship",
    )(*state)


def merge_kernel(group, resp_len, lengths, acc, top, total, other, stats, out):
    slots = out.shape[0]
    slot = lax.broadcasted_iota(jnp.int32, (slots, 128), 0)
    alive = slot % resp_len < live_of(lengths, slot, resp_len, slots // resp_len)
    for head in range(group):
        at = pl.ds(head * slots, slots)
        columns = slice(head * 128, (head + 1) * 128)
        shape = (slots, 128)
        other_top = jnp.broadcast_to(stats[:, head * 16 : head * 16 + 1], shape)
        place = (group + head) * 16
        other_total = jnp.broadcast_to(stats[:, place : place + 1], shape)
        peak = jnp.maximum(top[at, :], other_top)
        own = jnp.exp2(top[at, :] - peak)
        share = jnp.exp2(other_top - peak) * other_total
        accum = acc[at, :] * own + other[:, columns].astype(jnp.float32) * share
        result = jnp.where(alive, accum / (total[at, :] * own + share), 0.0)
        out[:, columns] = result.astype(jnp.bfloat16)


def merge(group, resp_len, lengths, state, other, stats):
    return pl.pallas_call(
        functools.partial(merge_kernel, group, resp_len),
        in_specs=[SMEM] + [VMEM] * 5,
        out_specs=VMEM,
        out_shape=jax.ShapeDtypeStruct(other.shape, jnp.bfloat16),
        compiler_params=params(),
        name="merge",
    )(lengths, *state, other, stats)


def project_kernel(near, core, own, first, second, far, w_own, w_first, w_second, w_mine, w_other, out):
    depth = w_mine.shape[0] // 2
    rows_at = slice(0, depth) if near else slice(depth, 2 * depth)

    def product(rows, weight):
        return jnp.dot(rows, weight, preferred_element_type=jnp.float32)

    total = product(own[...], w_own[...])
    total = total + product(first[...], w_first[...])
    total = total + product(second[...], w_second[...])
    for at, weight in ((core[0], w_mine), (1 - core[0], w_other)):
        rows = far[:, pl.ds(pl.multiple_of(at * depth, depth), depth)]
        total = total + product(rows, weight[rows_at, :])
    out[...] = total.astype(jnp.bfloat16)


def project(near, core, inputs, weights):
    return pl.pallas_call(
        functools.partial(project_kernel, near),
        in_specs=[SMEM] + [VMEM] * (len(inputs) + len(weights)),
        out_specs=VMEM,
        out_shape=jax.ShapeDtypeStruct((inputs[0].shape[0], weights[0].shape[1]), jnp.bfloat16),
        compiler_params=params(),
        name="project",
    )(jnp.reshape(core, (1,)), *inputs, *weights)


def per_device(queries, resp_keys, resp_values, prompt_keys, prompt_values, lengths, out_weight):
    head_size = prompt_keys.shape[1]
    slots = queries.shape[0]
    group = queries.shape[1] // head_size
    resp_len = slots // lengths.shape[0]
    scale = head_size ** (-0.5) * math.log2(math.e)
    z_size = lax.axis_size("z")
    x_size = lax.axis_size("x")
    core = lax.axis_index("core")
    x_at = lax.axis_index("x")
    yl_at = lax.axis_index("yl")

    swap_core = lambda v: lax.ppermute(v, "core", ring(2, 1))
    swap_yh = lambda v: lax.ppermute(v, "yh", ring(2, 1))
    swap_yl = lambda v: lax.ppermute(v, "yl", ring(2, 1))
    z_hop = lambda v: lax.ppermute(v, ("z", "core"), opposite(z_size, 1))
    x_near = lambda v: lax.ppermute(v, ("core", "x"), opposite_x(x_size, 1))
    x_back = lambda v: lax.ppermute(v, ("core", "x"), opposite_x(x_size, -1))
    x_far = lambda v: lax.ppermute(v, "x", ring(x_size, 2))

    after = lax.optimization_barrier

    kv = after(jnp.concatenate([prompt_keys, prompt_values], 1))
    self_kv = jnp.concatenate([resp_keys, resp_values], 1)
    half = kv.shape[0]
    full = 2 * half
    kv_core = swap_core(kv)
    q_core = swap_core(queries)
    kv_y = swap_yh(kv)
    pair = jnp.concatenate([kv, kv_core], 0)
    a_1 = z_hop(pair)

    share = out_weight.shape[1] // (x_size * 2)
    depth = out_weight.shape[0] // 2

    def columns(x_to, block, start=0, count=2 * depth):
        at = ((yl_at if block == 0 else 1 - yl_at) * x_size + x_to) * share
        return lax.dynamic_slice(out_weight, (start, at), (count, share))

    x_next = (x_at + jnp.where(core == 0, 1, x_size - 1)) % x_size
    x_after = (x_at + 2) % x_size
    w_far = jnp.concatenate([columns(x_after, block, core * depth, depth) for block in (0, 1)], 0)
    w_near = [columns(x_next, block) for block in (0, 1)]
    queries, pair, w_far, w_near = after((queries, pair, w_far, w_near))
    w_far = x_near(w_far)
    w_near = [x_near(w) for w in w_near]

    query_sets = [queries, q_core]
    run = functools.partial(attend, scale, group, resp_len)

    def step(states, *blocks):
        return run(query_sets, blocks, states)

    def ordered(states, *arrays):
        flat, arrays = after((states, arrays))
        return flat, *arrays

    states = run(query_sets, [(pair, half)], None, (lengths, self_kv))
    states, a_1 = ordered(states, a_1)
    a_2 = z_hop(a_1)
    states, kv_y = ordered(states, kv_y)
    kv_y_core = swap_core(kv_y)
    states = step(states, (a_1, full))
    states, kv_y, kv_y_core = ordered(states, kv_y, kv_y_core)
    b_1 = z_hop(jnp.concatenate([kv_y, kv_y_core], 0))
    states = step(states, (kv_y, half))
    states, a_2, w_far = ordered(states, a_2, w_far)
    w_far = x_near(w_far)
    a_3 = z_hop(a_2)
    b_2 = swap_yh(a_2)
    states = step(states, (a_2, full))
    states, b_1 = ordered(states, b_1)
    states = step(states, (b_1, full))
    states, a_3, w_near[1] = ordered(states, a_3, w_near[1])
    a_4 = z_hop(a_3[:half])
    states = step(states, (a_3, full))
    states, b_2, a_4 = ordered(states, b_2, a_4)
    b_3 = z_hop(b_2)
    b_4 = swap_yh(a_4)
    states = step(states, (b_2, full), (a_4, half))
    states, b_3, b_4, w_near[0] = ordered(states, b_3, b_4, w_near[0])
    last = [(b_3, full), (b_4, half)]
    theirs = run([q_core], last, [states[1]])[0]
    sent, stats = ship(group, theirs)
    own, sent, stats, w_far = ordered(states[0], sent, stats, w_far)
    got, got_stats = swap_core(sent), swap_core(stats)
    own = run([queries], last, [own])[0]
    attended = merge(group, resp_len, lengths, own, got, got_stats)

    w_back = [swap_core(w) for w in w_near]
    w_other = swap_core(w_far)
    gathered = [attended, x_near(attended), x_back(attended), x_far(attended)]

    def product(block):
        weights = [columns(x_at, block), w_near[block], w_back[block], w_far, w_other]
        return project(block == 0, core, gathered, weights)

    away = product(1)
    arrived = swap_yl(away)
    kept = product(0)
    return (kept.astype(jnp.float32) + arrived.astype(jnp.float32)).astype(jnp.bfloat16)


def solution(mesh):
    fine = Mesh(mesh.devices.reshape(8, 2, 2, 2, 4), ("z", "yh", "core", "yl", "x"))
    resp, head = ("z", "yh", "core"), ("yl", "x")
    return jax.shard_map(
        per_device,
        mesh=fine,
        in_specs=(P(resp, head),) * 5 + (P(resp), P(head, None)),
        out_specs=P(resp, head),
        check_vma=False,
    )
```

```python
import functools
import math

import jax
import jax.numpy as jnp
from jax import lax
from jax.experimental import pallas as pl
from jax.experimental.pallas import tpu as pltpu
from jax.sharding import Mesh, PartitionSpec as P

NEG = -1e30
NT = (((1,), (1,)), ((), ()))


def ring(size, step):
    return [(i, (i + step) % size) for i in range(size)]


def opposite(size, step):
    pairs = []
    for place in range(size):
        pairs.append((2 * place, 2 * ((place + step) % size)))
        pairs.append((2 * place + 1, 2 * ((place - step) % size) + 1))
    return pairs


def opposite_x(size, step):
    forward = [(i, (i + step) % size) for i in range(size)]
    backward = [(size + i, size + (i - step) % size) for i in range(size)]
    return forward + backward


def lanes(x, width):
    return x if width == x.shape[1] else jnp.concatenate([x] * (width // x.shape[1]), 1)


def with_ones(values):
    return jnp.concatenate([values, jnp.ones((values.shape[0], 128), jnp.bfloat16)], 1)


def fold(tiles, scale, query, blocks, read, write, extra=None):
    keys = [block[:, :128] for block in blocks]
    values = [with_ones(block[:, 128:]) for block in blocks]

    def score(tile):
        return [
            lax.dot_general(query(tile), key, NT, preferred_element_type=jnp.float32)
            for key in keys
        ]

    def finish(item):
        tile, pairs, shrink, top, old = item
        total = None
        for weight, value in pairs:
            term = jnp.dot(weight, value, preferred_element_type=jnp.float32)
            total = term if total is None else total + term
        accum, count = total[:, :128], total[:, 128:]
        if old is not None:
            accum = accum + old[0] * shrink
            count = count + old[2] * shrink
        write(tile, accum, top, count)

    upcoming = score(tiles[0])
    waiting = None
    for place, tile in enumerate(tiles):
        scores, sides = upcoming, values
        if place + 1 < len(tiles):
            upcoming = score(tiles[place + 1])
        if waiting is not None:
            finish(waiting)
        own = extra(tile) if extra is not None else None
        if own is not None:
            scores, sides = scores + [own[0]], sides + [own[1]]
        peak = None
        for part in scores:
            for at in range(0, part.shape[1], 128):
                column = part[:, at : at + 128]
                peak = column if peak is None else jnp.maximum(peak, column)
        top = jnp.broadcast_to(jnp.max(peak, 1, keepdims=True), peak.shape) * scale
        old = read(tile)
        shrink = None
        if old is not None:
            top = jnp.maximum(top, old[1])
            shrink = jnp.exp2(old[1] - top)
        weights = [
            jnp.exp2(part * scale - lanes(top, part.shape[1])).astype(jnp.bfloat16)
            for part in scores
        ]
        waiting = (tile, list(zip(weights, sides)), shrink, top, old)
    finish(waiting)


def live_of(lengths, index, resp_len, count):
    live = jnp.zeros(index.shape, jnp.int32)
    for response in range(count):
        live = jnp.where(index // resp_len == response, lengths[response], live)
    return live


def attend_kernel(scale, group, resp_len, sets, rows_of, first, with_self, *refs):
    refs = list(refs)
    lengths, own_keys, own_values = [refs.pop(0) for _ in range(3)] if with_self else [None] * 3
    queries = [refs.pop(0) for _ in range(sets)]
    blocks = [refs.pop(0)[:rows, :] for rows in rows_of]
    old = None if first else [[refs.pop(0) for _ in range(3)] for _ in range(sets)]
    new = [[refs.pop(0) for _ in range(3)] for _ in range(sets)]
    slots = queries[0].shape[0]
    tiles = [(index, head) for index in range(sets) for head in range(group)]

    def at(tile):
        return pl.ds(tile[1] * slots, slots)

    def query(tile):
        return queries[tile[0]][:, tile[1] * 128 : (tile[1] + 1) * 128]

    def read(tile):
        return None if first else [ref[at(tile), :] for ref in old[tile[0]]]

    def write(tile, *state):
        for ref, value in zip(new[tile[0]], state):
            ref[at(tile), :] = value

    extra = None
    if with_self:
        shape = (slots, slots)
        slot = lax.broadcasted_iota(jnp.int32, shape, 0)
        other = lax.broadcasted_iota(jnp.int32, shape, 1)
        keep = (slot // resp_len == other // resp_len) & (other <= slot)
        keep = keep & (other % resp_len < live_of(lengths, other, resp_len, slots // resp_len))
        own_sums = with_ones(own_values[...])

        def extra(tile):
            scores = lax.dot_general(
                query(tile), own_keys[...], NT, preferred_element_type=jnp.float32
            )
            return jnp.where(keep, scores, NEG), own_sums

    fold(tiles, scale, query, blocks, read, write, extra)


VMEM = pl.BlockSpec(memory_space=pltpu.VMEM)
SMEM = pl.BlockSpec(memory_space=pltpu.SMEM)


def params(mebibytes=32):
    return pltpu.CompilerParams(vmem_limit_bytes=mebibytes * 2**20)


def attend(scale, group, resp_len, queries, blocks, states=None, own=None, work=16):
    sets, slots = len(queries), queries[0].shape[0]
    rows = slots * group
    first = states is None
    operands = list(own or []) + list(queries) + [block for block, _ in blocks]
    keys = sum(count for _, count in blocks)
    state = jax.ShapeDtypeStruct((rows, 128), jnp.float32)
    aliases = {}
    if not first:
        aliases = {len(operands) + i: i for i in range(3 * sets)}
        operands += [array for one in states for array in one]
    specs = [VMEM] * len(operands)
    if own:
        specs[0] = SMEM
    out = pl.pallas_call(
        functools.partial(
            attend_kernel, scale, group, resp_len, sets, [count for _, count in blocks], first, bool(own)
        ),
        in_specs=specs,
        out_specs=[VMEM] * (3 * sets),
        out_shape=[state] * (3 * sets),
        input_output_aliases=aliases,
        compiler_params=params(),
        cost_estimate=pl.CostEstimate(
            flops=work * sets * rows * keys * 128, bytes_accessed=2**16, transcendentals=0
        ),
        name="attend",
    )(*operands)
    return [out[3 * i : 3 * i + 3] for i in range(sets)]


def ship_kernel(group, acc, top, total, out, stats):
    slots = out.shape[0]
    lane = lax.broadcasted_iota(jnp.int32, (slots, 128), 1) // 16
    packed = jnp.zeros((slots, 128), jnp.float32)
    for head in range(group):
        at = pl.ds(head * slots, slots)
        out[:, head * 128 : (head + 1) * 128] = (acc[at, :] / total[at, :]).astype(jnp.bfloat16)
        packed = jnp.where(lane == head, top[at, :], packed)
        packed = jnp.where(lane == group + head, total[at, :], packed)
    stats[...] = packed


def ship(group, state):
    slots = state[0].shape[0] // group
    return pl.pallas_call(
        functools.partial(ship_kernel, group),
        in_specs=[VMEM] * 3,
        out_specs=[VMEM] * 2,
        out_shape=[
            jax.ShapeDtypeStruct((slots, group * 128), jnp.bfloat16),
            jax.ShapeDtypeStruct((slots, 128), jnp.float32),
        ],
        compiler_params=params(),
        name="ship",
    )(*state)


def merge_kernel(group, resp_len, lengths, acc, top, total, other, stats, *outs):
    slots = other.shape[0]
    part = slots // len(outs)
    slot = lax.broadcasted_iota(jnp.int32, (slots, 128), 0)
    alive = slot % resp_len < live_of(lengths, slot, resp_len, slots // resp_len)
    for head in range(group):
        at = pl.ds(head * slots, slots)
        columns = slice(head * 128, (head + 1) * 128)
        shape = (slots, 128)
        other_top = jnp.broadcast_to(stats[:, head * 16 : head * 16 + 1], shape)
        place = (group + head) * 16
        other_total = jnp.broadcast_to(stats[:, place : place + 1], shape)
        peak = jnp.maximum(top[at, :], other_top)
        own = jnp.exp2(top[at, :] - peak)
        share = jnp.exp2(other_top - peak) * other_total
        accum = acc[at, :] * own + other[:, columns].astype(jnp.float32) * share
        result = jnp.where(alive, accum / (total[at, :] * own + share), 0.0)
        for index, out in enumerate(outs):
            out[:, columns] = result[index * part : (index + 1) * part].astype(jnp.bfloat16)


def merge(group, resp_len, lengths, state, other, stats):
    return pl.pallas_call(
        functools.partial(merge_kernel, group, resp_len),
        in_specs=[SMEM] + [VMEM] * 5,
        out_specs=[VMEM] * 2,
        out_shape=[jax.ShapeDtypeStruct((other.shape[0] // 2, other.shape[1]), jnp.bfloat16)] * 2,
        compiler_params=params(),
        name="merge",
    )(lengths, *state, other, stats)


def cut_kernel(places, weight, near, far, own, sems):
    rows, width = weight.shape[0], near.shape[1]
    depth = rows // 2
    copies = []
    for block in range(2):
        for out, count, start, column in (
            (near, rows, 0, places[block]),
            (far, depth, places[6], places[2 + block]),
            (own, rows, 0, places[4 + block]),
        ):
            source = weight.at[
                pl.ds(pl.multiple_of(start, depth), count),
                pl.ds(pl.multiple_of(column, width), width),
            ]
            target = out.at[pl.ds(block * count, count), :]
            copies.append(pltpu.make_async_copy(source, target, sems.at[len(copies)]))
    for copy in copies:
        copy.start()
    for copy in copies:
        copy.wait()


def cut(places, weight, width):
    rows = weight.shape[0]
    shapes = [jax.ShapeDtypeStruct((count, width), weight.dtype) for count in (2 * rows, rows, 2 * rows)]
    return pl.pallas_call(
        cut_kernel,
        in_specs=[SMEM, pl.BlockSpec(memory_space=pltpu.HBM)],
        out_specs=[VMEM] * 3,
        out_shape=shapes,
        scratch_shapes=[pltpu.SemaphoreType.DMA((6,))],
        compiler_params=params(46),
        name="cut",
    )(places, weight)


def project_kernel(block, core, own, first, second, far, w_own, w_first, w_second, w_mine, w_other, out):
    rows = w_own.shape[0] // 2
    depth = rows // 2

    def product(left, weight):
        return jnp.dot(left, weight, preferred_element_type=jnp.float32)

    total = None
    for left, weight in ((own, w_own), (first, w_first), (second, w_second)):
        term = product(left[...], weight[block * rows : (block + 1) * rows, :])
        total = term if total is None else total + term
    for at, weight in ((core[0], w_mine), (1 - core[0], w_other)):
        left = far[:, pl.ds(pl.multiple_of(at * depth, depth), depth)]
        total = total + product(left, weight[block * depth : (block + 1) * depth, :])
    out[...] = total.astype(jnp.bfloat16)


def project(block, core, inputs, weights):
    return pl.pallas_call(
        functools.partial(project_kernel, block),
        in_specs=[SMEM] + [VMEM] * (len(inputs) + len(weights)),
        out_specs=VMEM,
        out_shape=jax.ShapeDtypeStruct((inputs[0].shape[0], weights[0].shape[1]), jnp.bfloat16),
        compiler_params=params(),
        name="project",
    )(jnp.reshape(core, (1,)), *inputs, *weights)


def per_device(queries, resp_keys, resp_values, prompt_keys, prompt_values, lengths, out_weight):
    head_size = prompt_keys.shape[1]
    slots = queries.shape[0]
    group = queries.shape[1] // head_size
    resp_len = slots // lengths.shape[0]
    scale = head_size ** (-0.5) * math.log2(math.e)
    z_size = lax.axis_size("z")
    x_size = lax.axis_size("x")
    core = lax.axis_index("core")
    x_at = lax.axis_index("x")
    yl_at = lax.axis_index("yl")

    swap_core = lambda v: lax.ppermute(v, "core", ring(2, 1))
    swap_yh = lambda v: lax.ppermute(v, "yh", ring(2, 1))
    swap_yl = lambda v: lax.ppermute(v, "yl", ring(2, 1))
    z_hop = lambda v: lax.ppermute(v, ("z", "core"), opposite(z_size, 1))
    x_near = lambda v: lax.ppermute(v, ("core", "x"), opposite_x(x_size, 1))
    x_back = lambda v: lax.ppermute(v, ("core", "x"), opposite_x(x_size, -1))
    x_far = lambda v: lax.ppermute(v, "x", ring(x_size, 2))

    after = lax.optimization_barrier

    half = prompt_keys.shape[0]
    full = 2 * half
    keys_core, values_core = swap_core(prompt_keys), swap_core(prompt_values)
    q_core = swap_core(queries)
    kv = after(jnp.concatenate([prompt_keys, prompt_values], 1))
    kv_y = swap_yh(kv)
    pair = jnp.concatenate([kv, jnp.concatenate([keys_core, values_core], 1)], 0)
    pair = after(pair)
    a_1 = z_hop(pair)

    share = out_weight.shape[1] // (x_size * 2)
    x_next = (x_at + jnp.where(core == 0, 1, x_size - 1)) % x_size
    x_after = (x_at + 2) % x_size
    places = [
        (yl * x_size + x_to) * share for x_to in (x_next, x_after, x_at) for yl in (yl_at, 1 - yl_at)
    ]
    places = jnp.stack(places + [core * (out_weight.shape[0] // 2)]).astype(jnp.int32)

    query_sets = [queries, q_core]
    run = functools.partial(attend, scale, group, resp_len)

    def step(states, *blocks):
        return run(query_sets, blocks, states)

    def ordered(states, *arrays):
        flat, arrays = after((states, arrays))
        return flat, *arrays

    theirs = run([q_core], [(pair, half)], work=8)
    theirs, pair = ordered(theirs, pair)
    states = run([queries], [(pair, half)], None, (lengths, resp_keys, resp_values), work=8) + theirs
    states, places = ordered(states, places)
    w_near, w_far, w_own = cut(places, out_weight, share)
    w_far = x_near(w_far)
    states, a_1 = ordered(states, a_1)
    a_2 = z_hop(a_1)
    b_1 = swap_yh(a_1)
    states = run(query_sets, [(a_1, full)], states, work=32)
    states, kv_y, w_near = ordered(states, kv_y, w_near)
    w_near = x_near(w_near)
    states = run(query_sets, [(kv_y, half)], states, work=32)
    states, a_2 = ordered(states, a_2)
    a_3 = z_hop(a_2)
    b_2 = swap_yh(a_2)
    states = step(states, (a_2, full))
    states, b_1 = ordered(states, b_1)
    states = step(states, (b_1, full))
    states, a_3, w_far = ordered(states, a_3, w_far)
    w_far = x_near(w_far)
    a_4 = z_hop(a_3[:half])
    states = step(states, (a_3, full))
    states, b_2, a_4 = ordered(states, b_2, a_4)
    b_3 = z_hop(b_2)
    b_4 = swap_yh(a_4)
    states = run(query_sets, [(b_2, full), (a_4, half)], states, work=6)
    states, b_3, b_4, w_near = ordered(states, b_3, b_4, w_near)
    w_back = swap_core(w_near)
    last = [(b_3, full), (b_4, half)]
    theirs = run([q_core], last, [states[1]])[0]
    sent, stats = ship(group, theirs)
    own, sent, stats = ordered(states[0], sent, stats)
    got, got_stats = swap_core(sent), swap_core(stats)
    own = run([queries], last, [own])[0]
    attended = merge(group, resp_len, lengths, own, got, got_stats)

    attended, w_far = after((attended, w_far))
    w_other = swap_core(w_far)
    gathered = [[rows, x_near(rows), x_back(rows), x_far(rows)] for rows in attended]
    weights = [w_own, w_near, w_back, w_far, w_other]
    away = [project(1, core, rows, weights) for rows in gathered]
    arrived = [swap_yl(rows) for rows in away]
    kept = [project(0, core, rows, weights) for rows in gathered]
    kept, arrived = jnp.concatenate(kept, 0), jnp.concatenate(arrived, 0)
    return (kept.astype(jnp.float32) + arrived.astype(jnp.float32)).astype(jnp.bfloat16)


def solution(mesh):
    fine = Mesh(mesh.devices.reshape(8, 2, 2, 2, 4), ("z", "yh", "core", "yl", "x"))
    resp, head = ("z", "yh", "core"), ("yl", "x")
    return jax.shard_map(
        per_device,
        mesh=fine,
        in_specs=(P(resp, head),) * 5 + (P(resp), P(head, None)),
        out_specs=P(resp, head),
        check_vma=False,
    )
```

```python
import functools
import math

import jax
import jax.numpy as jnp
from jax import lax
from jax.experimental import pallas as pl
from jax.experimental.pallas import tpu as pltpu
from jax.sharding import Mesh, PartitionSpec as P

NEG = -1e30
NT = (((1,), (1,)), ((), ()))


def ring(size, step):
    return [(i, (i + step) % size) for i in range(size)]


def opposite(size, step):
    pairs = []
    for place in range(size):
        pairs.append((2 * place, 2 * ((place + step) % size)))
        pairs.append((2 * place + 1, 2 * ((place - step) % size) + 1))
    return pairs


def opposite_x(size, step):
    forward = [(i, (i + step) % size) for i in range(size)]
    backward = [(size + i, size + (i - step) % size) for i in range(size)]
    return forward + backward


def lanes(x, width):
    return x if width == x.shape[1] else jnp.concatenate([x] * (width // x.shape[1]), 1)


def with_ones(values):
    return jnp.concatenate([values, jnp.ones((values.shape[0], 128), jnp.bfloat16)], 1)


def fold(tiles, scale, query, blocks, read, write, extra=None):
    keys = [block[:, :128] for block in blocks]
    values = [with_ones(block[:, 128:]) for block in blocks]

    def score(tile):
        return [
            lax.dot_general(query(tile), key, NT, preferred_element_type=jnp.float32)
            for key in keys
        ]

    def finish(item):
        tile, pairs, shrink, top, old = item
        total = None
        for weight, value in pairs:
            term = jnp.dot(weight, value, preferred_element_type=jnp.float32)
            total = term if total is None else total + term
        accum, count = total[:, :128], total[:, 128:]
        if old is not None:
            accum = accum + old[0] * shrink
            count = count + old[2] * shrink
        write(tile, accum, top, count)

    upcoming = score(tiles[0])
    waiting = None
    for place, tile in enumerate(tiles):
        scores, sides = upcoming, values
        if place + 1 < len(tiles):
            upcoming = score(tiles[place + 1])
        if waiting is not None:
            finish(waiting)
        own = extra(tile) if extra is not None else None
        if own is not None:
            scores, sides = scores + [own[0]], sides + [own[1]]
        peak = None
        for part in scores:
            for at in range(0, part.shape[1], 128):
                column = part[:, at : at + 128]
                peak = column if peak is None else jnp.maximum(peak, column)
        top = jnp.broadcast_to(jnp.max(peak, 1, keepdims=True), peak.shape) * scale
        old = read(tile)
        shrink = None
        if old is not None:
            top = jnp.maximum(top, old[1])
            shrink = jnp.exp2(old[1] - top)
        weights = [
            jnp.exp2(part * scale - lanes(top, part.shape[1])).astype(jnp.bfloat16)
            for part in scores
        ]
        waiting = (tile, list(zip(weights, sides)), shrink, top, old)
    finish(waiting)


def live_of(lengths, index, resp_len, count):
    live = jnp.zeros(index.shape, jnp.int32)
    for response in range(count):
        live = jnp.where(index // resp_len == response, lengths[response], live)
    return live


def attend_kernel(scale, group, resp_len, sets, rows_of, first, with_self, *refs):
    refs = list(refs)
    lengths, own_keys, own_values = [refs.pop(0) for _ in range(3)] if with_self else [None] * 3
    queries = [refs.pop(0) for _ in range(sets)]
    blocks = [refs.pop(0)[:rows, :] for rows in rows_of]
    old = None if first else [[refs.pop(0) for _ in range(3)] for _ in range(sets)]
    new = [[refs.pop(0) for _ in range(3)] for _ in range(sets)]
    slots = queries[0].shape[0]
    turns = 2

    def at(tile):
        return pl.ds(pl.multiple_of(tile[1] * slots, slots), slots)

    def query(tile):
        return queries[tile[0]][:, pl.ds(pl.multiple_of(tile[1] * 128, 128), 128)]

    def read(tile):
        return None if first else [ref[at(tile), :] for ref in old[tile[0]]]

    def write(tile, *state):
        for ref, value in zip(new[tile[0]], state):
            ref[at(tile), :] = value

    extra = None
    if with_self:
        shape = (slots, slots)
        slot = lax.broadcasted_iota(jnp.int32, shape, 0)
        other = lax.broadcasted_iota(jnp.int32, shape, 1)
        keep = (slot // resp_len == other // resp_len) & (other <= slot)
        keep = keep & (other % resp_len < live_of(lengths, other, resp_len, slots // resp_len))
        own_sums = with_ones(own_values[...])

        def extra(tile):
            scores = lax.dot_general(
                query(tile), own_keys[...], NT, preferred_element_type=jnp.float32
            )
            return jnp.where(keep, scores, NEG), own_sums

    def turn(index, _):
        heads = [index * (group // turns) + head for head in range(group // turns)]
        tiles = [(place, head) for place in range(sets) for head in heads]
        fold(tiles, scale, query, blocks, read, write, extra)
        return 0

    if turns == 1:
        turn(0, 0)
    else:
        lax.fori_loop(0, turns, turn, 0)


VMEM = pl.BlockSpec(memory_space=pltpu.VMEM)
SMEM = pl.BlockSpec(memory_space=pltpu.SMEM)


def params(mebibytes=32):
    return pltpu.CompilerParams(vmem_limit_bytes=mebibytes * 2**20)


def attend(scale, group, resp_len, queries, blocks, states=None, own=None, work=16):
    sets, slots = len(queries), queries[0].shape[0]
    rows = slots * group
    first = states is None
    operands = list(own or []) + list(queries) + [block for block, _ in blocks]
    keys = sum(count for _, count in blocks)
    state = jax.ShapeDtypeStruct((rows, 128), jnp.float32)
    aliases = {}
    if not first:
        aliases = {len(operands) + i: i for i in range(3 * sets)}
        operands += [array for one in states for array in one]
    specs = [VMEM] * len(operands)
    if own:
        specs[0] = SMEM
    out = pl.pallas_call(
        functools.partial(
            attend_kernel, scale, group, resp_len, sets, [count for _, count in blocks], first, bool(own)
        ),
        in_specs=specs,
        out_specs=[VMEM] * (3 * sets),
        out_shape=[state] * (3 * sets),
        input_output_aliases=aliases,
        compiler_params=params(),
        cost_estimate=pl.CostEstimate(
            flops=work * sets * rows * keys * 128, bytes_accessed=2**16, transcendentals=0
        ),
        name="attend",
    )(*operands)
    return [out[3 * i : 3 * i + 3] for i in range(sets)]


def ship_kernel(group, acc, top, total, out, stats):
    slots = out.shape[0]
    lane = lax.broadcasted_iota(jnp.int32, (slots, 128), 1) // 16
    packed = jnp.zeros((slots, 128), jnp.float32)
    for head in range(group):
        at = pl.ds(head * slots, slots)
        out[:, head * 128 : (head + 1) * 128] = (acc[at, :] / total[at, :]).astype(jnp.bfloat16)
        packed = jnp.where(lane == head, top[at, :], packed)
        packed = jnp.where(lane == group + head, total[at, :], packed)
    stats[...] = packed


def ship(group, state):
    slots = state[0].shape[0] // group
    return pl.pallas_call(
        functools.partial(ship_kernel, group),
        in_specs=[VMEM] * 3,
        out_specs=[VMEM] * 2,
        out_shape=[
            jax.ShapeDtypeStruct((slots, group * 128), jnp.bfloat16),
            jax.ShapeDtypeStruct((slots, 128), jnp.float32),
        ],
        compiler_params=params(),
        name="ship",
    )(*state)


def merge_kernel(group, resp_len, lengths, acc, top, total, other, stats, *outs):
    slots = other.shape[0]
    part = slots // len(outs)
    slot = lax.broadcasted_iota(jnp.int32, (slots, 128), 0)
    alive = slot % resp_len < live_of(lengths, slot, resp_len, slots // resp_len)
    for head in range(group):
        at = pl.ds(head * slots, slots)
        columns = slice(head * 128, (head + 1) * 128)
        shape = (slots, 128)
        other_top = jnp.broadcast_to(stats[:, head * 16 : head * 16 + 1], shape)
        place = (group + head) * 16
        other_total = jnp.broadcast_to(stats[:, place : place + 1], shape)
        peak = jnp.maximum(top[at, :], other_top)
        own = jnp.exp2(top[at, :] - peak)
        share = jnp.exp2(other_top - peak) * other_total
        accum = acc[at, :] * own + other[:, columns].astype(jnp.float32) * share
        result = jnp.where(alive, accum / (total[at, :] * own + share), 0.0)
        for index, out in enumerate(outs):
            out[:, columns] = result[index * part : (index + 1) * part].astype(jnp.bfloat16)


def merge(group, resp_len, lengths, state, other, stats):
    return pl.pallas_call(
        functools.partial(merge_kernel, group, resp_len),
        in_specs=[SMEM] + [VMEM] * 5,
        out_specs=[VMEM] * 2,
        out_shape=[jax.ShapeDtypeStruct((other.shape[0] // 2, other.shape[1]), jnp.bfloat16)] * 2,
        compiler_params=params(),
        name="merge",
    )(lengths, *state, other, stats)


def cut_kernel(places, weight, near, far, own, sems):
    rows, width = weight.shape[0], near.shape[1]
    depth = rows // 2
    copies = []
    for block in range(2):
        for out, count, start, column in (
            (near, rows, 0, places[block]),
            (far, depth, places[6], places[2 + block]),
            (own, rows, 0, places[4 + block]),
        ):
            source = weight.at[
                pl.ds(pl.multiple_of(start, depth), count),
                pl.ds(pl.multiple_of(column, width), width),
            ]
            target = out.at[pl.ds(block * count, count), :]
            copies.append(pltpu.make_async_copy(source, target, sems.at[len(copies)]))
    for copy in copies:
        copy.start()
    for copy in copies:
        copy.wait()


def cut(places, weight, width):
    rows = weight.shape[0]
    shapes = [jax.ShapeDtypeStruct((count, width), weight.dtype) for count in (2 * rows, rows, 2 * rows)]
    return pl.pallas_call(
        cut_kernel,
        in_specs=[SMEM, pl.BlockSpec(memory_space=pltpu.HBM)],
        out_specs=[VMEM] * 3,
        out_shape=shapes,
        scratch_shapes=[pltpu.SemaphoreType.DMA((6,))],
        compiler_params=params(46),
        name="cut",
    )(places, weight)


def project_kernel(block, core, own, first, second, far, w_own, w_first, w_second, w_mine, w_other, out):
    rows = w_own.shape[0] // 2
    depth = rows // 2

    def product(left, weight):
        return jnp.dot(left, weight, preferred_element_type=jnp.float32)

    total = None
    for left, weight in ((own, w_own), (first, w_first), (second, w_second)):
        term = product(left[...], weight[block * rows : (block + 1) * rows, :])
        total = term if total is None else total + term
    for at, weight in ((core[0], w_mine), (1 - core[0], w_other)):
        left = far[:, pl.ds(pl.multiple_of(at * depth, depth), depth)]
        total = total + product(left, weight[block * depth : (block + 1) * depth, :])
    out[...] = total.astype(jnp.bfloat16)


def project(block, core, inputs, weights):
    return pl.pallas_call(
        functools.partial(project_kernel, block),
        in_specs=[SMEM] + [VMEM] * (len(inputs) + len(weights)),
        out_specs=VMEM,
        out_shape=jax.ShapeDtypeStruct((inputs[0].shape[0], weights[0].shape[1]), jnp.bfloat16),
        compiler_params=params(),
        name="project",
    )(jnp.reshape(core, (1,)), *inputs, *weights)


def per_device(queries, resp_keys, resp_values, prompt_keys, prompt_values, lengths, out_weight):
    head_size = prompt_keys.shape[1]
    slots = queries.shape[0]
    group = queries.shape[1] // head_size
    resp_len = slots // lengths.shape[0]
    scale = head_size ** (-0.5) * math.log2(math.e)
    z_size = lax.axis_size("z")
    x_size = lax.axis_size("x")
    core = lax.axis_index("core")
    x_at = lax.axis_index("x")
    yl_at = lax.axis_index("yl")

    swap_core = lambda v: lax.ppermute(v, "core", ring(2, 1))
    swap_yh = lambda v: lax.ppermute(v, "yh", ring(2, 1))
    swap_yl = lambda v: lax.ppermute(v, "yl", ring(2, 1))
    z_hop = lambda v: lax.ppermute(v, ("z", "core"), opposite(z_size, 1))
    x_near = lambda v: lax.ppermute(v, ("core", "x"), opposite_x(x_size, 1))
    x_back = lambda v: lax.ppermute(v, ("core", "x"), opposite_x(x_size, -1))
    x_far = lambda v: lax.ppermute(v, "x", ring(x_size, 2))

    after = lax.optimization_barrier

    half = prompt_keys.shape[0]
    full = 2 * half
    keys_core, values_core = swap_core(prompt_keys), swap_core(prompt_values)
    q_core = swap_core(queries)
    kv = after(jnp.concatenate([prompt_keys, prompt_values], 1))
    kv_y = swap_yh(kv)
    pair = jnp.concatenate([kv, jnp.concatenate([keys_core, values_core], 1)], 0)
    pair = after(pair)
    a_1 = z_hop(pair)

    share = out_weight.shape[1] // (x_size * 2)
    x_next = (x_at + jnp.where(core == 0, 1, x_size - 1)) % x_size
    x_after = (x_at + 2) % x_size
    places = [
        (yl * x_size + x_to) * share for x_to in (x_next, x_after, x_at) for yl in (yl_at, 1 - yl_at)
    ]
    places = jnp.stack(places + [core * (out_weight.shape[0] // 2)]).astype(jnp.int32)

    query_sets = [queries, q_core]
    run = functools.partial(attend, scale, group, resp_len)

    def step(states, *blocks):
        return run(query_sets, blocks, states)

    def ordered(states, *arrays):
        flat, arrays = after((states, arrays))
        return flat, *arrays

    theirs = run([q_core], [(pair, half)], work=8)
    theirs, pair = ordered(theirs, pair)
    states = run([queries], [(pair, half)], None, (lengths, resp_keys, resp_values), work=8) + theirs
    states, places = ordered(states, places)
    w_near, w_far, w_own = cut(places, out_weight, share)
    w_far = x_near(w_far)
    states, a_1 = ordered(states, a_1)
    a_2 = z_hop(a_1)
    b_1 = swap_yh(a_1)
    states = run(query_sets, [(a_1, full)], states, work=32)
    states, kv_y, w_near = ordered(states, kv_y, w_near)
    w_near = x_near(w_near)
    states = run(query_sets, [(kv_y, half)], states, work=32)
    states, a_2 = ordered(states, a_2)
    a_3 = z_hop(a_2)
    b_2 = swap_yh(a_2)
    states = step(states, (a_2, full))
    states, b_1 = ordered(states, b_1)
    states = step(states, (b_1, full))
    states, a_3, w_far = ordered(states, a_3, w_far)
    w_far = x_near(w_far)
    a_4 = z_hop(a_3[:half])
    states = step(states, (a_3, full))
    states, b_2, a_4 = ordered(states, b_2, a_4)
    b_3 = z_hop(b_2)
    b_4 = swap_yh(a_4)
    states = run(query_sets, [(b_2, full), (a_4, half)], states, work=6)
    states, b_3, b_4, w_near = ordered(states, b_3, b_4, w_near)
    w_back = swap_core(w_near)
    last = [(b_3, full), (b_4, half)]
    theirs = run([q_core], last, [states[1]])[0]
    sent, stats = ship(group, theirs)
    own, sent, stats = ordered(states[0], sent, stats)
    got, got_stats = swap_core(sent), swap_core(stats)
    own = run([queries], last, [own])[0]
    attended = merge(group, resp_len, lengths, own, got, got_stats)

    attended, w_far = after((attended, w_far))
    w_other = swap_core(w_far)
    gathered = [[rows, x_near(rows), x_back(rows), x_far(rows)] for rows in attended]
    weights = [w_own, w_near, w_back, w_far, w_other]
    away = [project(1, core, rows, weights) for rows in gathered]
    arrived = [swap_yl(rows) for rows in away]
    kept = [project(0, core, rows, weights) for rows in gathered]
    kept, arrived = jnp.concatenate(kept, 0), jnp.concatenate(arrived, 0)
    return (kept.astype(jnp.float32) + arrived.astype(jnp.float32)).astype(jnp.bfloat16)


def solution(mesh):
    fine = Mesh(mesh.devices.reshape(8, 2, 2, 2, 4), ("z", "yh", "core", "yl", "x"))
    resp, head = ("z", "yh", "core"), ("yl", "x")
    return jax.shard_map(
        per_device,
        mesh=fine,
        in_specs=(P(resp, head),) * 5 + (P(resp), P(head, None)),
        out_specs=P(resp, head),
        check_vma=False,
    )
```

```python
import functools
import math

import jax
import jax.numpy as jnp
from jax import lax
from jax.experimental import pallas as pl
from jax.experimental.pallas import tpu as pltpu
from jax.sharding import Mesh, PartitionSpec as P

NEG = -1e30
NT = (((1,), (1,)), ((), ()))


def ring(size, step):
    return [(i, (i + step) % size) for i in range(size)]


def opposite(size, step):
    pairs = []
    for place in range(size):
        pairs.append((2 * place, 2 * ((place + step) % size)))
        pairs.append((2 * place + 1, 2 * ((place - step) % size) + 1))
    return pairs


def opposite_x(size, step):
    forward = [(i, (i + step) % size) for i in range(size)]
    backward = [(size + i, size + (i - step) % size) for i in range(size)]
    return forward + backward


def lanes(x, width):
    return x if width == x.shape[1] else jnp.concatenate([x] * (width // x.shape[1]), 1)


def with_ones(values):
    return jnp.concatenate([values, jnp.ones((values.shape[0], 128), jnp.bfloat16)], 1)


def fold(tiles, scale, query, blocks, read, write, extra=None):
    keys = [block[:, :128] for block in blocks]
    values = [with_ones(block[:, 128:]) for block in blocks]

    def score(tile):
        return [
            lax.dot_general(query(tile), key, NT, preferred_element_type=jnp.float32)
            for key in keys
        ]

    def finish(item):
        tile, pairs, shrink, top, old = item
        total = None
        for weight, value in pairs:
            term = jnp.dot(weight, value, preferred_element_type=jnp.float32)
            total = term if total is None else total + term
        accum, count = total[:, :128], total[:, 128:]
        if old is not None:
            accum = accum + old[0] * shrink
            count = count + old[2] * shrink
        write(tile, accum, top, count)

    upcoming = score(tiles[0])
    waiting = None
    for place, tile in enumerate(tiles):
        scores, sides = upcoming, values
        if place + 1 < len(tiles):
            upcoming = score(tiles[place + 1])
        if waiting is not None:
            finish(waiting)
        own = extra(tile) if extra is not None else None
        if own is not None:
            scores, sides = scores + [own[0]], sides + [own[1]]
        peak = None
        for part in scores:
            for at in range(0, part.shape[1], 128):
                column = part[:, at : at + 128]
                peak = column if peak is None else jnp.maximum(peak, column)
        top = jnp.broadcast_to(jnp.max(peak, 1, keepdims=True), peak.shape) * scale
        old = read(tile)
        shrink = None
        if old is not None:
            top = jnp.maximum(top, old[1])
            shrink = jnp.exp2(old[1] - top)
        weights = [
            jnp.exp2(part * scale - lanes(top, part.shape[1])).astype(jnp.bfloat16)
            for part in scores
        ]
        waiting = (tile, list(zip(weights, sides)), shrink, top, old)
    finish(waiting)


def live_of(lengths, index, resp_len, count):
    live = jnp.zeros(index.shape, jnp.int32)
    for response in range(count):
        live = jnp.where(index // resp_len == response, lengths[response], live)
    return live


def attend_kernel(scale, group, resp_len, sets, rows_of, first, with_self, *refs):
    refs = list(refs)
    lengths, own_keys, own_values = [refs.pop(0) for _ in range(3)] if with_self else [None] * 3
    queries = [refs.pop(0) for _ in range(sets)]
    blocks = [refs.pop(0)[:rows, :] for rows in rows_of]
    old = None if first else [[refs.pop(0) for _ in range(3)] for _ in range(sets)]
    new = [[refs.pop(0) for _ in range(3)] for _ in range(sets)]
    slots = queries[0].shape[0]
    turns = 2

    def at(tile):
        return pl.ds(pl.multiple_of(tile[1] * slots, slots), slots)

    def query(tile):
        return queries[tile[0]][:, pl.ds(pl.multiple_of(tile[1] * 128, 128), 128)]

    def read(tile):
        return None if first else [ref[at(tile), :] for ref in old[tile[0]]]

    def write(tile, *state):
        for ref, value in zip(new[tile[0]], state):
            ref[at(tile), :] = value

    extra = None
    if with_self:
        shape = (slots, slots)
        slot = lax.broadcasted_iota(jnp.int32, shape, 0)
        other = lax.broadcasted_iota(jnp.int32, shape, 1)
        keep = (slot // resp_len == other // resp_len) & (other <= slot)
        keep = keep & (other % resp_len < live_of(lengths, other, resp_len, slots // resp_len))
        own_sums = with_ones(own_values[...])

        def extra(tile):
            scores = lax.dot_general(
                query(tile), own_keys[...], NT, preferred_element_type=jnp.float32
            )
            return jnp.where(keep, scores, NEG), own_sums

    def turn(index, _):
        heads = [index * (group // turns) + head for head in range(group // turns)]
        tiles = [(place, head) for place in range(sets) for head in heads]
        fold(tiles, scale, query, blocks, read, write, extra)
        return 0

    if turns == 1:
        turn(0, 0)
    else:
        lax.fori_loop(0, turns, turn, 0)


VMEM = pl.BlockSpec(memory_space=pltpu.VMEM)
SMEM = pl.BlockSpec(memory_space=pltpu.SMEM)


def params(mebibytes=32):
    return pltpu.CompilerParams(vmem_limit_bytes=mebibytes * 2**20)


def attend(scale, group, resp_len, queries, blocks, states=None, own=None, work=16):
    sets, slots = len(queries), queries[0].shape[0]
    rows = slots * group
    first = states is None
    operands = list(own or []) + list(queries) + [block for block, _ in blocks]
    keys = sum(count for _, count in blocks)
    state = jax.ShapeDtypeStruct((rows, 128), jnp.float32)
    aliases = {}
    if not first:
        aliases = {len(operands) + i: i for i in range(3 * sets)}
        operands += [array for one in states for array in one]
    specs = [VMEM] * len(operands)
    if own:
        specs[0] = SMEM
    out = pl.pallas_call(
        functools.partial(
            attend_kernel, scale, group, resp_len, sets, [count for _, count in blocks], first, bool(own)
        ),
        in_specs=specs,
        out_specs=[VMEM] * (3 * sets),
        out_shape=[state] * (3 * sets),
        input_output_aliases=aliases,
        compiler_params=params(),
        cost_estimate=pl.CostEstimate(
            flops=work * sets * rows * keys * 128, bytes_accessed=2**16, transcendentals=0
        ),
        name="attend",
    )(*operands)
    return [out[3 * i : 3 * i + 3] for i in range(sets)]


def ship_kernel(group, acc, top, total, out, stats):
    slots = out.shape[0]
    lane = lax.broadcasted_iota(jnp.int32, (slots, 128), 1) // 16
    packed = jnp.zeros((slots, 128), jnp.float32)
    for head in range(group):
        at = pl.ds(head * slots, slots)
        out[:, head * 128 : (head + 1) * 128] = (acc[at, :] / total[at, :]).astype(jnp.bfloat16)
        packed = jnp.where(lane == head, top[at, :], packed)
        packed = jnp.where(lane == group + head, total[at, :], packed)
    stats[...] = packed


def ship(group, state):
    slots = state[0].shape[0] // group
    return pl.pallas_call(
        functools.partial(ship_kernel, group),
        in_specs=[VMEM] * 3,
        out_specs=[VMEM] * 2,
        out_shape=[
            jax.ShapeDtypeStruct((slots, group * 128), jnp.bfloat16),
            jax.ShapeDtypeStruct((slots, 128), jnp.float32),
        ],
        compiler_params=params(),
        name="ship",
    )(*state)


def merge_kernel(group, resp_len, lengths, acc, top, total, other, stats, *outs):
    slots = other.shape[0]
    part = slots // len(outs)
    slot = lax.broadcasted_iota(jnp.int32, (slots, 128), 0)
    alive = slot % resp_len < live_of(lengths, slot, resp_len, slots // resp_len)
    for head in range(group):
        at = pl.ds(head * slots, slots)
        columns = slice(head * 128, (head + 1) * 128)
        shape = (slots, 128)
        other_top = jnp.broadcast_to(stats[:, head * 16 : head * 16 + 1], shape)
        place = (group + head) * 16
        other_total = jnp.broadcast_to(stats[:, place : place + 1], shape)
        peak = jnp.maximum(top[at, :], other_top)
        own = jnp.exp2(top[at, :] - peak)
        share = jnp.exp2(other_top - peak) * other_total
        accum = acc[at, :] * own + other[:, columns].astype(jnp.float32) * share
        result = jnp.where(alive, accum / (total[at, :] * own + share), 0.0)
        for index, out in enumerate(outs):
            out[:, columns] = result[index * part : (index + 1) * part].astype(jnp.bfloat16)


def merge(group, resp_len, lengths, state, other, stats):
    return pl.pallas_call(
        functools.partial(merge_kernel, group, resp_len),
        in_specs=[SMEM] + [VMEM] * 5,
        out_specs=[VMEM] * 2,
        out_shape=[jax.ShapeDtypeStruct((other.shape[0] // 2, other.shape[1]), jnp.bfloat16)] * 2,
        compiler_params=params(),
        name="merge",
    )(lengths, *state, other, stats)


def cut_kernel(places, weight, near, far, own, sems):
    rows, width = weight.shape[0], near.shape[1]
    depth = rows // 2
    copies = []
    for block in range(2):
        for out, count, start, column in (
            (near, rows, 0, places[block]),
            (far, depth, places[6], places[2 + block]),
            (own, rows, 0, places[4 + block]),
        ):
            source = weight.at[
                pl.ds(pl.multiple_of(start, depth), count),
                pl.ds(pl.multiple_of(column, width), width),
            ]
            target = out.at[pl.ds(block * count, count), :]
            copies.append(pltpu.make_async_copy(source, target, sems.at[len(copies)]))
    for copy in copies:
        copy.start()
    for copy in copies:
        copy.wait()


def cut(places, weight, width):
    rows = weight.shape[0]
    shapes = [jax.ShapeDtypeStruct((count, width), weight.dtype) for count in (2 * rows, rows, 2 * rows)]
    return pl.pallas_call(
        cut_kernel,
        in_specs=[SMEM, pl.BlockSpec(memory_space=pltpu.HBM)],
        out_specs=[VMEM] * 3,
        out_shape=shapes,
        scratch_shapes=[pltpu.SemaphoreType.DMA((6,))],
        compiler_params=params(46),
        cost_estimate=pl.CostEstimate(flops=4096 * 2**20, bytes_accessed=2**20, transcendentals=0),
        name="cut",
    )(places, weight)


def project_kernel(block, core, own, first, second, far, w_own, w_first, w_second, w_mine, w_other, out):
    rows = w_own.shape[0] // 2
    depth = rows // 2

    def product(left, weight):
        return jnp.dot(left, weight, preferred_element_type=jnp.float32)

    total = None
    for left, weight in ((own, w_own), (first, w_first), (second, w_second)):
        term = product(left[...], weight[block * rows : (block + 1) * rows, :])
        total = term if total is None else total + term
    for at, weight in ((core[0], w_mine), (1 - core[0], w_other)):
        left = far[:, pl.ds(pl.multiple_of(at * depth, depth), depth)]
        total = total + product(left, weight[block * depth : (block + 1) * depth, :])
    out[...] = total.astype(jnp.bfloat16)


def project(block, core, inputs, weights):
    return pl.pallas_call(
        functools.partial(project_kernel, block),
        in_specs=[SMEM] + [VMEM] * (len(inputs) + len(weights)),
        out_specs=VMEM,
        out_shape=jax.ShapeDtypeStruct((inputs[0].shape[0], weights[0].shape[1]), jnp.bfloat16),
        compiler_params=params(),
        name="project",
    )(jnp.reshape(core, (1,)), *inputs, *weights)


def per_device(queries, resp_keys, resp_values, prompt_keys, prompt_values, lengths, out_weight):
    head_size = prompt_keys.shape[1]
    slots = queries.shape[0]
    group = queries.shape[1] // head_size
    resp_len = slots // lengths.shape[0]
    scale = head_size ** (-0.5) * math.log2(math.e)
    z_size = lax.axis_size("z")
    x_size = lax.axis_size("x")
    core = lax.axis_index("core")
    x_at = lax.axis_index("x")
    yl_at = lax.axis_index("yl")

    swap_core = lambda v: lax.ppermute(v, "core", ring(2, 1))
    swap_yh = lambda v: lax.ppermute(v, "yh", ring(2, 1))
    swap_yl = lambda v: lax.ppermute(v, "yl", ring(2, 1))
    z_hop = lambda v: lax.ppermute(v, ("z", "core"), opposite(z_size, 1))
    x_near = lambda v: lax.ppermute(v, ("core", "x"), opposite_x(x_size, 1))
    x_back = lambda v: lax.ppermute(v, ("core", "x"), opposite_x(x_size, -1))
    x_far = lambda v: lax.ppermute(v, "x", ring(x_size, 2))

    after = lax.optimization_barrier

    half = prompt_keys.shape[0]
    full = 2 * half
    keys_core, values_core = swap_core(prompt_keys), swap_core(prompt_values)
    q_core = swap_core(queries)
    kv = after(jnp.concatenate([prompt_keys, prompt_values], 1))
    kv_y = swap_yh(kv)
    pair = jnp.concatenate([kv, jnp.concatenate([keys_core, values_core], 1)], 0)
    pair = after(pair)
    a_1 = z_hop(pair)

    share = out_weight.shape[1] // (x_size * 2)
    x_next = (x_at + jnp.where(core == 0, 1, x_size - 1)) % x_size
    x_after = (x_at + 2) % x_size
    places = [
        (yl * x_size + x_to) * share for x_to in (x_next, x_after, x_at) for yl in (yl_at, 1 - yl_at)
    ]
    places = jnp.stack(places + [core * (out_weight.shape[0] // 2)]).astype(jnp.int32)

    query_sets = [queries, q_core]
    run = functools.partial(attend, scale, group, resp_len)

    def step(states, *blocks):
        return run(query_sets, blocks, states)

    def ordered(states, *arrays):
        flat, arrays = after((states, arrays))
        return flat, *arrays

    places, pair = after((places, pair))
    w_near, w_far, w_own = cut(places, out_weight, share)
    w_far, pair = after((w_far, pair))
    w_far = x_near(w_far)
    theirs = run([q_core], [(pair, half)], work=8)
    theirs, pair = ordered(theirs, pair)
    states = run([queries], [(pair, half)], None, (lengths, resp_keys, resp_values), work=8) + theirs
    states, a_1 = ordered(states, a_1)
    a_2 = z_hop(a_1)
    b_1 = swap_yh(a_1)
    states = run(query_sets, [(a_1, full)], states, work=32)
    states, kv_y, w_near = ordered(states, kv_y, w_near)
    w_near = x_near(w_near)
    states = run(query_sets, [(kv_y, half)], states, work=32)
    states, a_2 = ordered(states, a_2)
    a_3 = z_hop(a_2)
    b_2 = swap_yh(a_2)
    states = step(states, (a_2, full))
    states, b_1 = ordered(states, b_1)
    states = step(states, (b_1, full))
    states, a_3, w_far = ordered(states, a_3, w_far)
    w_far = x_near(w_far)
    a_4 = z_hop(a_3[:half])
    states = step(states, (a_3, full))
    states, b_2 = ordered(states, b_2)
    b_3 = z_hop(b_2)
    states, a_4, b_2 = ordered(states, a_4, b_2)
    b_4 = swap_yh(a_4)
    states = run(query_sets, [(b_2, full), (a_4, half)], states, work=16)
    states, b_3, b_4, w_near = ordered(states, b_3, b_4, w_near)
    w_back = swap_core(w_near)
    last = [(b_3, full), (b_4, half)]
    theirs = run([q_core], last, [states[1]])[0]
    sent, stats = ship(group, theirs)
    own, sent, stats = ordered(states[0], sent, stats)
    got, got_stats = swap_core(sent), swap_core(stats)
    own = run([queries], last, [own])[0]
    attended = merge(group, resp_len, lengths, own, got, got_stats)

    attended, w_far = after((attended, w_far))
    w_other = swap_core(w_far)
    gathered = [[rows, x_near(rows), x_back(rows), x_far(rows)] for rows in attended]
    weights = [w_own, w_near, w_back, w_far, w_other]
    away = [project(1, core, rows, weights) for rows in gathered]
    arrived = [swap_yl(rows) for rows in away]
    kept = [project(0, core, rows, weights) for rows in gathered]
    kept, arrived = jnp.concatenate(kept, 0), jnp.concatenate(arrived, 0)
    return (kept.astype(jnp.float32) + arrived.astype(jnp.float32)).astype(jnp.bfloat16)


def solution(mesh):
    fine = Mesh(mesh.devices.reshape(8, 2, 2, 2, 4), ("z", "yh", "core", "yl", "x"))
    resp, head = ("z", "yh", "core"), ("yl", "x")
    return jax.shard_map(
        per_device,
        mesh=fine,
        in_specs=(P(resp, head),) * 5 + (P(resp), P(head, None)),
        out_specs=P(resp, head),
        check_vma=False,
    )
```

```python
import functools
import math

import jax
import jax.numpy as jnp
from jax import lax
from jax.experimental import pallas as pl
from jax.experimental.pallas import tpu as pltpu
from jax.sharding import Mesh, PartitionSpec as P

NEG = -1e30
NT = (((1,), (1,)), ((), ()))


def ring(size, step):
    return [(i, (i + step) % size) for i in range(size)]


def opposite(size, step):
    pairs = []
    for place in range(size):
        pairs.append((2 * place, 2 * ((place + step) % size)))
        pairs.append((2 * place + 1, 2 * ((place - step) % size) + 1))
    return pairs


def opposite_x(size, step):
    forward = [(i, (i + step) % size) for i in range(size)]
    backward = [(size + i, size + (i - step) % size) for i in range(size)]
    return forward + backward


def lanes(x, width):
    return x if width == x.shape[1] else jnp.concatenate([x] * (width // x.shape[1]), 1)


def with_ones(values):
    return jnp.concatenate([values, jnp.ones((values.shape[0], 128), jnp.bfloat16)], 1)


def fold(tiles, scale, query, blocks, read, write, extra=None):
    keys = [block[:, :128] for block in blocks]
    values = [with_ones(block[:, 128:]) for block in blocks]

    def score(tile):
        return [
            lax.dot_general(query(tile), key, NT, preferred_element_type=jnp.float32)
            for key in keys
        ]

    def finish(item):
        tile, pairs, shrink, top, old = item
        total = None
        for weight, value in pairs:
            term = jnp.dot(weight, value, preferred_element_type=jnp.float32)
            total = term if total is None else total + term
        accum, count = total[:, :128], total[:, 128:]
        if old is not None:
            accum = accum + old[0] * shrink
            count = count + old[2] * shrink
        write(tile, accum, top, count)

    upcoming = score(tiles[0])
    waiting = None
    for place, tile in enumerate(tiles):
        scores, sides = upcoming, values
        if place + 1 < len(tiles):
            upcoming = score(tiles[place + 1])
        if waiting is not None:
            finish(waiting)
        own = extra(tile) if extra is not None else None
        if own is not None:
            scores, sides = scores + [own[0]], sides + [own[1]]
        peak = None
        for part in scores:
            for at in range(0, part.shape[1], 128):
                column = part[:, at : at + 128]
                peak = column if peak is None else jnp.maximum(peak, column)
        top = jnp.broadcast_to(jnp.max(peak, 1, keepdims=True), peak.shape) * scale
        old = read(tile)
        shrink = None
        if old is not None:
            top = jnp.maximum(top, old[1])
            shrink = jnp.exp2(old[1] - top)
        weights = [
            jnp.exp2(part * scale - lanes(top, part.shape[1])).astype(jnp.bfloat16)
            for part in scores
        ]
        waiting = (tile, list(zip(weights, sides)), shrink, top, old)
    finish(waiting)


def live_of(lengths, index, resp_len, count):
    live = jnp.zeros(index.shape, jnp.int32)
    for response in range(count):
        live = jnp.where(index // resp_len == response, lengths[response], live)
    return live


def attend_kernel(scale, group, resp_len, sets, rows_of, first, with_self, *refs):
    refs = list(refs)
    lengths, own_keys, own_values = [refs.pop(0) for _ in range(3)] if with_self else [None] * 3
    queries = [refs.pop(0) for _ in range(sets)]
    blocks = [refs.pop(0)[:rows, :] for rows in rows_of]
    old = None if first else [[refs.pop(0) for _ in range(3)] for _ in range(sets)]
    new = [[refs.pop(0) for _ in range(3)] for _ in range(sets)]
    slots = queries[0].shape[0]
    turns = 2

    def at(tile):
        return pl.ds(pl.multiple_of(tile[1] * slots, slots), slots)

    def query(tile):
        return queries[tile[0]][:, pl.ds(pl.multiple_of(tile[1] * 128, 128), 128)]

    def read(tile):
        return None if first else [ref[at(tile), :] for ref in old[tile[0]]]

    def write(tile, *state):
        for ref, value in zip(new[tile[0]], state):
            ref[at(tile), :] = value

    extra = None
    if with_self:
        shape = (slots, slots)
        slot = lax.broadcasted_iota(jnp.int32, shape, 0)
        other = lax.broadcasted_iota(jnp.int32, shape, 1)
        keep = (slot // resp_len == other // resp_len) & (other <= slot)
        keep = keep & (other % resp_len < live_of(lengths, other, resp_len, slots // resp_len))
        own_sums = with_ones(own_values[...])

        def extra(tile):
            scores = lax.dot_general(
                query(tile), own_keys[...], NT, preferred_element_type=jnp.float32
            )
            return jnp.where(keep, scores, NEG), own_sums

    def turn(index, _):
        heads = [index * (group // turns) + head for head in range(group // turns)]
        tiles = [(place, head) for place in range(sets) for head in heads]
        fold(tiles, scale, query, blocks, read, write, extra)
        return 0

    if turns == 1:
        turn(0, 0)
    else:
        lax.fori_loop(0, turns, turn, 0)


VMEM = pl.BlockSpec(memory_space=pltpu.VMEM)
SMEM = pl.BlockSpec(memory_space=pltpu.SMEM)


def params(mebibytes=32):
    return pltpu.CompilerParams(vmem_limit_bytes=mebibytes * 2**20)


def attend(scale, group, resp_len, queries, blocks, states=None, own=None, work=16):
    sets, slots = len(queries), queries[0].shape[0]
    rows = slots * group
    first = states is None
    operands = list(own or []) + list(queries) + [block for block, _ in blocks]
    keys = sum(count for _, count in blocks)
    state = jax.ShapeDtypeStruct((rows, 128), jnp.float32)
    aliases = {}
    if not first:
        aliases = {len(operands) + i: i for i in range(3 * sets)}
        operands += [array for one in states for array in one]
    specs = [VMEM] * len(operands)
    if own:
        specs[0] = SMEM
    out = pl.pallas_call(
        functools.partial(
            attend_kernel, scale, group, resp_len, sets, [count for _, count in blocks], first, bool(own)
        ),
        in_specs=specs,
        out_specs=[VMEM] * (3 * sets),
        out_shape=[state] * (3 * sets),
        input_output_aliases=aliases,
        compiler_params=params(),
        cost_estimate=pl.CostEstimate(
            flops=work * sets * rows * keys * 128, bytes_accessed=2**16, transcendentals=0
        ),
        name="attend",
    )(*operands)
    return [out[3 * i : 3 * i + 3] for i in range(sets)]


def ship_kernel(group, acc, top, total, out, stats):
    slots = out.shape[0]
    lane = lax.broadcasted_iota(jnp.int32, (slots, 128), 1) // 16
    packed = jnp.zeros((slots, 128), jnp.float32)
    for head in range(group):
        at = pl.ds(head * slots, slots)
        out[:, head * 128 : (head + 1) * 128] = (acc[at, :] / total[at, :]).astype(jnp.bfloat16)
        packed = jnp.where(lane == head, top[at, :], packed)
        packed = jnp.where(lane == group + head, total[at, :], packed)
    stats[...] = packed


def ship(group, state):
    slots = state[0].shape[0] // group
    return pl.pallas_call(
        functools.partial(ship_kernel, group),
        in_specs=[VMEM] * 3,
        out_specs=[VMEM] * 2,
        out_shape=[
            jax.ShapeDtypeStruct((slots, group * 128), jnp.bfloat16),
            jax.ShapeDtypeStruct((slots, 128), jnp.float32),
        ],
        compiler_params=params(),
        name="ship",
    )(*state)


def merge_kernel(group, resp_len, lengths, acc, top, total, other, stats, *outs):
    slots = other.shape[0]
    part = slots // len(outs)
    slot = lax.broadcasted_iota(jnp.int32, (slots, 128), 0)
    alive = slot % resp_len < live_of(lengths, slot, resp_len, slots // resp_len)
    for head in range(group):
        at = pl.ds(head * slots, slots)
        columns = slice(head * 128, (head + 1) * 128)
        shape = (slots, 128)
        other_top = jnp.broadcast_to(stats[:, head * 16 : head * 16 + 1], shape)
        place = (group + head) * 16
        other_total = jnp.broadcast_to(stats[:, place : place + 1], shape)
        peak = jnp.maximum(top[at, :], other_top)
        own = jnp.exp2(top[at, :] - peak)
        share = jnp.exp2(other_top - peak) * other_total
        accum = acc[at, :] * own + other[:, columns].astype(jnp.float32) * share
        result = jnp.where(alive, accum / (total[at, :] * own + share), 0.0)
        for index, out in enumerate(outs):
            out[:, columns] = result[index * part : (index + 1) * part].astype(jnp.bfloat16)


def merge(group, resp_len, lengths, state, other, stats):
    return pl.pallas_call(
        functools.partial(merge_kernel, group, resp_len),
        in_specs=[SMEM] + [VMEM] * 5,
        out_specs=[VMEM] * 2,
        out_shape=[jax.ShapeDtypeStruct((other.shape[0] // 2, other.shape[1]), jnp.bfloat16)] * 2,
        compiler_params=params(),
        name="merge",
    )(lengths, *state, other, stats)


def cut_kernel(places, weight, near, far, own, sems):
    rows, width = weight.shape[0], near.shape[1]
    depth = rows // 2
    copies = []
    for block in range(2):
        for out, count, start, column in (
            (near, rows, 0, places[block]),
            (far, depth, places[6], places[2 + block]),
            (own, rows, 0, places[4 + block]),
        ):
            source = weight.at[
                pl.ds(pl.multiple_of(start, depth), count),
                pl.ds(pl.multiple_of(column, width), width),
            ]
            target = out.at[pl.ds(block * count, count), :]
            copies.append(pltpu.make_async_copy(source, target, sems.at[len(copies)]))
    for copy in copies:
        copy.start()
    for copy in copies:
        copy.wait()


def cut(places, weight, width):
    rows = weight.shape[0]
    shapes = [jax.ShapeDtypeStruct((count, width), weight.dtype) for count in (2 * rows, rows, 2 * rows)]
    return pl.pallas_call(
        cut_kernel,
        in_specs=[SMEM, pl.BlockSpec(memory_space=pltpu.HBM)],
        out_specs=[VMEM] * 3,
        out_shape=shapes,
        scratch_shapes=[pltpu.SemaphoreType.DMA((6,))],
        compiler_params=params(46),
        cost_estimate=pl.CostEstimate(flops=4096 * 2**20, bytes_accessed=2**20, transcendentals=0),
        name="cut",
    )(places, weight)


def project_kernel(block, core, own, first, second, far, w_own, w_first, w_second, w_mine, w_other, out):
    rows = w_own.shape[0] // 2
    depth = rows // 2

    def product(left, weight):
        return jnp.dot(left, weight, preferred_element_type=jnp.float32)

    total = None
    for left, weight in ((own, w_own), (first, w_first), (second, w_second)):
        term = product(left[...], weight[block * rows : (block + 1) * rows, :])
        total = term if total is None else total + term
    for at, weight in ((core[0], w_mine), (1 - core[0], w_other)):
        left = far[:, pl.ds(pl.multiple_of(at * depth, depth), depth)]
        total = total + product(left, weight[block * depth : (block + 1) * depth, :])
    out[...] = total.astype(jnp.bfloat16)


def project(block, core, inputs, weights):
    return pl.pallas_call(
        functools.partial(project_kernel, block),
        in_specs=[SMEM] + [VMEM] * (len(inputs) + len(weights)),
        out_specs=VMEM,
        out_shape=jax.ShapeDtypeStruct((inputs[0].shape[0], weights[0].shape[1]), jnp.bfloat16),
        compiler_params=params(),
        name="project",
    )(jnp.reshape(core, (1,)), *inputs, *weights)


def per_device(queries, resp_keys, resp_values, prompt_keys, prompt_values, lengths, out_weight):
    head_size = prompt_keys.shape[1]
    slots = queries.shape[0]
    group = queries.shape[1] // head_size
    resp_len = slots // lengths.shape[0]
    scale = head_size ** (-0.5) * math.log2(math.e)
    z_size = lax.axis_size("z")
    x_size = lax.axis_size("x")
    core = lax.axis_index("core")
    x_at = lax.axis_index("x")
    yl_at = lax.axis_index("yl")

    swap_core = lambda v: lax.ppermute(v, "core", ring(2, 1))
    swap_yh = lambda v: lax.ppermute(v, "yh", ring(2, 1))
    swap_yl = lambda v: lax.ppermute(v, "yl", ring(2, 1))
    z_hop = lambda v: lax.ppermute(v, ("z", "core"), opposite(z_size, 1))
    x_near = lambda v: lax.ppermute(v, ("core", "x"), opposite_x(x_size, 1))
    x_back = lambda v: lax.ppermute(v, ("core", "x"), opposite_x(x_size, -1))

    after = lax.optimization_barrier

    half = prompt_keys.shape[0]
    full = 2 * half
    keys_core, values_core = swap_core(prompt_keys), swap_core(prompt_values)
    q_core = swap_core(queries)
    kv = after(jnp.concatenate([prompt_keys, prompt_values], 1))
    kv_y = swap_yh(kv)
    pair = jnp.concatenate([kv, jnp.concatenate([keys_core, values_core], 1)], 0)
    pair = after(pair)
    a_1 = z_hop(pair)

    share = out_weight.shape[1] // (x_size * 2)
    x_next = (x_at + jnp.where(core == 0, 1, x_size - 1)) % x_size
    x_after = (x_at + 2) % x_size
    places = [
        (yl * x_size + x_to) * share for x_to in (x_next, x_after, x_at) for yl in (yl_at, 1 - yl_at)
    ]
    places = jnp.stack(places + [core * (out_weight.shape[0] // 2)]).astype(jnp.int32)

    query_sets = [queries, q_core]
    run = functools.partial(attend, scale, group, resp_len)

    def step(states, *blocks):
        return run(query_sets, blocks, states)

    def ordered(states, *arrays):
        flat, arrays = after((states, arrays))
        return flat, *arrays

    places, pair = after((places, pair))
    w_near, w_far, w_own = cut(places, out_weight, share)
    w_far, pair = after((w_far, pair))
    w_far = x_near(w_far)
    theirs = run([q_core], [(pair, half)], work=8)
    theirs, pair = ordered(theirs, pair)
    states = run([queries], [(pair, half)], None, (lengths, resp_keys, resp_values), work=8) + theirs
    states, a_1 = ordered(states, a_1)
    a_2 = z_hop(a_1)
    b_1 = swap_yh(a_1)
    states = run(query_sets, [(a_1, full)], states, work=32)
    states, kv_y, w_near = ordered(states, kv_y, w_near)
    w_near = x_near(w_near)
    states = run(query_sets, [(kv_y, half)], states, work=32)
    states, a_2 = ordered(states, a_2)
    a_3 = z_hop(a_2)
    b_2 = swap_yh(a_2)
    states = step(states, (a_2, full))
    states, b_1 = ordered(states, b_1)
    states = step(states, (b_1, full))
    states, a_3, w_far = ordered(states, a_3, w_far)
    w_far = x_near(w_far)
    a_4 = z_hop(a_3[:half])
    states = step(states, (a_3, full))
    states, b_2 = ordered(states, b_2)
    b_3 = z_hop(b_2)
    states, a_4, b_2 = ordered(states, a_4, b_2)
    b_4 = swap_yh(a_4)
    states = run(query_sets, [(b_2, full), (a_4, half)], states, work=16)
    states, b_3, b_4, w_near = ordered(states, b_3, b_4, w_near)
    w_back = swap_core(w_near)
    last = [(b_3, full), (b_4, half)]
    theirs = run([q_core], last, [states[1]])[0]
    sent, stats = ship(group, theirs)
    own, sent, stats = ordered(states[0], sent, stats)
    got, got_stats = swap_core(sent), swap_core(stats)
    own = run([queries], last, [own])[0]
    attended = merge(group, resp_len, lengths, own, got, got_stats)

    attended, w_far = after((attended, w_far))
    w_other = swap_core(w_far)
    gathered = []
    for rows in attended:
        near = x_near(rows)
        gathered.append([rows, near, x_back(rows), x_near(near)])
    weights = [w_own, w_near, w_back, w_far, w_other]
    away = [project(1, core, rows, weights) for rows in gathered]
    arrived = [swap_yl(rows) for rows in away]
    kept = [project(0, core, rows, weights) for rows in gathered]
    kept, arrived = jnp.concatenate(kept, 0), jnp.concatenate(arrived, 0)
    return (kept.astype(jnp.float32) + arrived.astype(jnp.float32)).astype(jnp.bfloat16)


def solution(mesh):
    fine = Mesh(mesh.devices.reshape(8, 2, 2, 2, 4), ("z", "yh", "core", "yl", "x"))
    resp, head = ("z", "yh", "core"), ("yl", "x")
    return jax.shard_map(
        per_device,
        mesh=fine,
        in_specs=(P(resp, head),) * 5 + (P(resp), P(head, None)),
        out_specs=P(resp, head),
        check_vma=False,
    )
```

```python
import functools
import math

import jax
import jax.numpy as jnp
from jax import lax
from jax.experimental import pallas as pl
from jax.experimental.pallas import tpu as pltpu
from jax.sharding import Mesh, PartitionSpec as P

NEG = -1e30
NT = (((1,), (1,)), ((), ()))


def ring(size, step):
    return [(i, (i + step) % size) for i in range(size)]


def opposite(size, step):
    pairs = []
    for place in range(size):
        pairs.append((2 * place, 2 * ((place + step) % size)))
        pairs.append((2 * place + 1, 2 * ((place - step) % size) + 1))
    return pairs


def opposite_x(size, step):
    forward = [(i, (i + step) % size) for i in range(size)]
    backward = [(size + i, size + (i - step) % size) for i in range(size)]
    return forward + backward


def lanes(x, width):
    return x if width == x.shape[1] else jnp.concatenate([x] * (width // x.shape[1]), 1)


def with_ones(values):
    return jnp.concatenate([values, jnp.ones((values.shape[0], 128), jnp.bfloat16)], 1)


def fold(tiles, scale, query, blocks, read, write, extra=None):
    keys = [block[:, :128] for block in blocks]
    values = [with_ones(block[:, 128:]) for block in blocks]

    def score(tile):
        return [
            lax.dot_general(query(tile), key, NT, preferred_element_type=jnp.float32)
            for key in keys
        ]

    def finish(item):
        tile, pairs, shrink, top, old = item
        total = None
        for weight, value in pairs:
            term = jnp.dot(weight, value, preferred_element_type=jnp.float32)
            total = term if total is None else total + term
        accum, count = total[:, :128], total[:, 128:]
        if old is not None:
            accum = accum + old[0] * shrink
            count = count + old[2] * shrink
        write(tile, accum, top, count)

    upcoming = score(tiles[0])
    waiting = None
    for place, tile in enumerate(tiles):
        scores, sides = upcoming, values
        if place + 1 < len(tiles):
            upcoming = score(tiles[place + 1])
        if waiting is not None:
            finish(waiting)
        own = extra(tile) if extra is not None else None
        if own is not None:
            scores, sides = scores + [own[0]], sides + [own[1]]
        peak = None
        for part in scores:
            for at in range(0, part.shape[1], 128):
                column = part[:, at : at + 128]
                peak = column if peak is None else jnp.maximum(peak, column)
        top = jnp.broadcast_to(jnp.max(peak, 1, keepdims=True), peak.shape) * scale
        old = read(tile)
        shrink = None
        if old is not None:
            top = jnp.maximum(top, old[1])
            shrink = jnp.exp2(old[1] - top)
        weights = [
            jnp.exp2(part * scale - lanes(top, part.shape[1])).astype(jnp.bfloat16)
            for part in scores
        ]
        waiting = (tile, list(zip(weights, sides)), shrink, top, old)
    finish(waiting)


def live_of(lengths, index, resp_len, count):
    live = jnp.zeros(index.shape, jnp.int32)
    for response in range(count):
        live = jnp.where(index // resp_len == response, lengths[response], live)
    return live


def attend_kernel(scale, group, resp_len, sets, rows_of, first, with_self, *refs):
    refs = list(refs)
    lengths, own_keys, own_values = [refs.pop(0) for _ in range(3)] if with_self else [None] * 3
    queries = [refs.pop(0) for _ in range(sets)]
    blocks = [refs.pop(0)[:rows, :] for rows in rows_of]
    old = None if first else [[refs.pop(0) for _ in range(3)] for _ in range(sets)]
    new = [[refs.pop(0) for _ in range(3)] for _ in range(sets)]
    slots = queries[0].shape[0]
    turns = 1 if first and not with_self else 2

    def at(tile):
        return pl.ds(pl.multiple_of(tile[1] * slots, slots), slots)

    def query(tile):
        return queries[tile[0]][:, pl.ds(pl.multiple_of(tile[1] * 128, 128), 128)]

    def read(tile):
        return None if first else [ref[at(tile), :] for ref in old[tile[0]]]

    def write(tile, *state):
        for ref, value in zip(new[tile[0]], state):
            ref[at(tile), :] = value

    extra = None
    if with_self:
        shape = (slots, slots)
        slot = lax.broadcasted_iota(jnp.int32, shape, 0)
        other = lax.broadcasted_iota(jnp.int32, shape, 1)
        keep = (slot // resp_len == other // resp_len) & (other <= slot)
        keep = keep & (other % resp_len < live_of(lengths, other, resp_len, slots // resp_len))
        own_sums = with_ones(own_values[...])

        def extra(tile):
            scores = lax.dot_general(
                query(tile), own_keys[...], NT, preferred_element_type=jnp.float32
            )
            return jnp.where(keep, scores, NEG), own_sums

    def turn(index, _):
        heads = [index * (group // turns) + head for head in range(group // turns)]
        tiles = [(place, head) for place in range(sets) for head in heads]
        fold(tiles, scale, query, blocks, read, write, extra)
        return 0

    if turns == 1:
        turn(0, 0)
    else:
        lax.fori_loop(0, turns, turn, 0)


VMEM = pl.BlockSpec(memory_space=pltpu.VMEM)
SMEM = pl.BlockSpec(memory_space=pltpu.SMEM)


def params(mebibytes=32):
    return pltpu.CompilerParams(vmem_limit_bytes=mebibytes * 2**20)


def attend(scale, group, resp_len, queries, blocks, states=None, own=None, work=16):
    sets, slots = len(queries), queries[0].shape[0]
    rows = slots * group
    first = states is None
    operands = list(own or []) + list(queries) + [block for block, _ in blocks]
    keys = sum(count for _, count in blocks)
    state = jax.ShapeDtypeStruct((rows, 128), jnp.float32)
    aliases = {}
    if not first:
        aliases = {len(operands) + i: i for i in range(3 * sets)}
        operands += [array for one in states for array in one]
    specs = [VMEM] * len(operands)
    if own:
        specs[0] = SMEM
    out = pl.pallas_call(
        functools.partial(
            attend_kernel, scale, group, resp_len, sets, [count for _, count in blocks], first, bool(own)
        ),
        in_specs=specs,
        out_specs=[VMEM] * (3 * sets),
        out_shape=[state] * (3 * sets),
        input_output_aliases=aliases,
        compiler_params=params(),
        cost_estimate=pl.CostEstimate(
            flops=work * sets * rows * keys * 128, bytes_accessed=2**16, transcendentals=0
        ),
        name="attend",
    )(*operands)
    return [out[3 * i : 3 * i + 3] for i in range(sets)]


def ship_kernel(group, acc, top, total, out, stats):
    slots = out.shape[0]
    lane = lax.broadcasted_iota(jnp.int32, (slots, 128), 1) // 16
    packed = jnp.zeros((slots, 128), jnp.float32)
    for head in range(group):
        at = pl.ds(head * slots, slots)
        out[:, head * 128 : (head + 1) * 128] = (acc[at, :] / total[at, :]).astype(jnp.bfloat16)
        packed = jnp.where(lane == head, top[at, :], packed)
        packed = jnp.where(lane == group + head, total[at, :], packed)
    stats[...] = packed


def ship(group, state):
    slots = state[0].shape[0] // group
    return pl.pallas_call(
        functools.partial(ship_kernel, group),
        in_specs=[VMEM] * 3,
        out_specs=[VMEM] * 2,
        out_shape=[
            jax.ShapeDtypeStruct((slots, group * 128), jnp.bfloat16),
            jax.ShapeDtypeStruct((slots, 128), jnp.float32),
        ],
        compiler_params=params(),
        name="ship",
    )(*state)


def merge_kernel(group, resp_len, lengths, acc, top, total, other, stats, *outs):
    slots = other.shape[0]
    part = slots // len(outs)
    slot = lax.broadcasted_iota(jnp.int32, (slots, 128), 0)
    alive = slot % resp_len < live_of(lengths, slot, resp_len, slots // resp_len)
    for head in range(group):
        at = pl.ds(head * slots, slots)
        columns = slice(head * 128, (head + 1) * 128)
        shape = (slots, 128)
        other_top = jnp.broadcast_to(stats[:, head * 16 : head * 16 + 1], shape)
        place = (group + head) * 16
        other_total = jnp.broadcast_to(stats[:, place : place + 1], shape)
        peak = jnp.maximum(top[at, :], other_top)
        own = jnp.exp2(top[at, :] - peak)
        share = jnp.exp2(other_top - peak) * other_total
        accum = acc[at, :] * own + other[:, columns].astype(jnp.float32) * share
        result = jnp.where(alive, accum / (total[at, :] * own + share), 0.0)
        for index, out in enumerate(outs):
            out[:, columns] = result[index * part : (index + 1) * part].astype(jnp.bfloat16)


def merge(group, resp_len, lengths, state, other, stats):
    return pl.pallas_call(
        functools.partial(merge_kernel, group, resp_len),
        in_specs=[SMEM] + [VMEM] * 5,
        out_specs=[VMEM] * 2,
        out_shape=[jax.ShapeDtypeStruct((other.shape[0] // 2, other.shape[1]), jnp.bfloat16)] * 2,
        compiler_params=params(),
        name="merge",
    )(lengths, *state, other, stats)


def cut_kernel(places, weight, near, far, own, sems):
    rows, width = weight.shape[0], near.shape[1]
    depth = rows // 2
    copies = []
    for block in range(2):
        for out, count, start, column in (
            (near, rows, 0, places[block]),
            (far, depth, places[6], places[2 + block]),
            (own, rows, 0, places[4 + block]),
        ):
            source = weight.at[
                pl.ds(pl.multiple_of(start, depth), count),
                pl.ds(pl.multiple_of(column, width), width),
            ]
            target = out.at[pl.ds(block * count, count), :]
            copies.append(pltpu.make_async_copy(source, target, sems.at[len(copies)]))
    for copy in copies:
        copy.start()
    for copy in copies:
        copy.wait()


def cut(places, weight, width):
    rows = weight.shape[0]
    shapes = [jax.ShapeDtypeStruct((count, width), weight.dtype) for count in (2 * rows, rows, 2 * rows)]
    return pl.pallas_call(
        cut_kernel,
        in_specs=[SMEM, pl.BlockSpec(memory_space=pltpu.HBM)],
        out_specs=[VMEM] * 3,
        out_shape=shapes,
        scratch_shapes=[pltpu.SemaphoreType.DMA((6,))],
        compiler_params=params(46),
        cost_estimate=pl.CostEstimate(flops=4096 * 2**20, bytes_accessed=2**20, transcendentals=0),
        name="cut",
    )(places, weight)


def project_kernel(block, core, own, first, second, far, w_own, w_first, w_second, w_mine, w_other, out):
    rows = w_own.shape[0] // 2
    depth = rows // 2

    def product(left, weight):
        return jnp.dot(left, weight, preferred_element_type=jnp.float32)

    total = None
    for left, weight in ((own, w_own), (first, w_first), (second, w_second)):
        term = product(left[...], weight[block * rows : (block + 1) * rows, :])
        total = term if total is None else total + term
    for at, weight in ((core[0], w_mine), (1 - core[0], w_other)):
        left = far[:, pl.ds(pl.multiple_of(at * depth, depth), depth)]
        total = total + product(left, weight[block * depth : (block + 1) * depth, :])
    out[...] = total.astype(jnp.bfloat16)


def project(block, core, inputs, weights):
    return pl.pallas_call(
        functools.partial(project_kernel, block),
        in_specs=[SMEM] + [VMEM] * (len(inputs) + len(weights)),
        out_specs=VMEM,
        out_shape=jax.ShapeDtypeStruct((inputs[0].shape[0], weights[0].shape[1]), jnp.bfloat16),
        compiler_params=params(),
        name="project",
    )(jnp.reshape(core, (1,)), *inputs, *weights)


def per_device(queries, resp_keys, resp_values, prompt_keys, prompt_values, lengths, out_weight):
    head_size = prompt_keys.shape[1]
    slots = queries.shape[0]
    group = queries.shape[1] // head_size
    resp_len = slots // lengths.shape[0]
    scale = head_size ** (-0.5) * math.log2(math.e)
    z_size = lax.axis_size("z")
    x_size = lax.axis_size("x")
    core = lax.axis_index("core")
    x_at = lax.axis_index("x")
    yl_at = lax.axis_index("yl")

    swap_core = lambda v: lax.ppermute(v, "core", ring(2, 1))
    swap_yh = lambda v: lax.ppermute(v, "yh", ring(2, 1))
    swap_yl = lambda v: lax.ppermute(v, "yl", ring(2, 1))
    z_hop = lambda v: lax.ppermute(v, ("z", "core"), opposite(z_size, 1))
    x_near = lambda v: lax.ppermute(v, ("core", "x"), opposite_x(x_size, 1))
    x_back = lambda v: lax.ppermute(v, ("core", "x"), opposite_x(x_size, -1))

    after = lax.optimization_barrier

    half = prompt_keys.shape[0]
    full = 2 * half
    keys_core, values_core = swap_core(prompt_keys), swap_core(prompt_values)
    q_core = swap_core(queries)
    kv = after(jnp.concatenate([prompt_keys, prompt_values], 1))
    kv_y = swap_yh(kv)
    pair = jnp.concatenate([kv, jnp.concatenate([keys_core, values_core], 1)], 0)
    pair = after(pair)
    a_1 = z_hop(pair)

    share = out_weight.shape[1] // (x_size * 2)
    x_next = (x_at + jnp.where(core == 0, 1, x_size - 1)) % x_size
    x_after = (x_at + 2) % x_size
    places = [
        (yl * x_size + x_to) * share for x_to in (x_next, x_after, x_at) for yl in (yl_at, 1 - yl_at)
    ]
    places = jnp.stack(places + [core * (out_weight.shape[0] // 2)]).astype(jnp.int32)

    query_sets = [queries, q_core]
    run = functools.partial(attend, scale, group, resp_len)

    def step(states, *blocks):
        return run(query_sets, blocks, states)

    def ordered(states, *arrays):
        flat, arrays = after((states, arrays))
        return flat, *arrays

    places, pair = after((places, pair))
    w_near, w_far, w_own = cut(places, out_weight, share)
    w_far, pair = after((w_far, pair))
    w_far = x_near(w_far)
    theirs = run([q_core], [(pair, half)], work=8)
    theirs, pair = ordered(theirs, pair)
    states = run([queries], [(pair, half)], None, (lengths, resp_keys, resp_values), work=8) + theirs
    states, a_1 = ordered(states, a_1)
    a_2 = z_hop(a_1)
    b_1 = swap_yh(a_1)
    states = run(query_sets, [(a_1, full)], states, work=32)
    states, kv_y, w_near = ordered(states, kv_y, w_near)
    w_near = x_near(w_near)
    states = run(query_sets, [(kv_y, half)], states, work=32)
    states, a_2 = ordered(states, a_2)
    a_3 = z_hop(a_2)
    b_2 = swap_yh(a_2)
    states = step(states, (a_2, full))
    states, b_1 = ordered(states, b_1)
    states = step(states, (b_1, full))
    states, a_3, w_far = ordered(states, a_3, w_far)
    w_far = x_near(w_far)
    a_4 = z_hop(a_3[:half])
    states = step(states, (a_3, full))
    states, b_2 = ordered(states, b_2)
    b_3 = z_hop(b_2)
    states, a_4, b_2 = ordered(states, a_4, b_2)
    b_4 = swap_yh(a_4)
    states = run(query_sets, [(b_2, full), (a_4, half)], states, work=16)
    states, b_3, b_4, w_near = ordered(states, b_3, b_4, w_near)
    w_back = swap_core(w_near)
    last = [(b_3, full), (b_4, half)]
    theirs = run([q_core], last, [states[1]])[0]
    sent, stats = ship(group, theirs)
    own, sent, stats = ordered(states[0], sent, stats)
    got, got_stats = swap_core(sent), swap_core(stats)
    own = run([queries], last, [own])[0]
    attended = merge(group, resp_len, lengths, own, got, got_stats)

    attended, w_far = after((attended, w_far))
    w_other = swap_core(w_far)
    gathered = []
    for rows in attended:
        near = x_near(rows)
        gathered.append([rows, near, x_back(rows), x_near(near)])
    weights = [w_own, w_near, w_back, w_far, w_other]
    away = [project(1, core, rows, weights) for rows in gathered]
    arrived = [swap_yl(rows) for rows in away]
    kept = [project(0, core, rows, weights) for rows in gathered]
    kept, arrived = jnp.concatenate(kept, 0), jnp.concatenate(arrived, 0)
    return (kept.astype(jnp.float32) + arrived.astype(jnp.float32)).astype(jnp.bfloat16)


def solution(mesh):
    fine = Mesh(mesh.devices.reshape(8, 2, 2, 2, 4), ("z", "yh", "core", "yl", "x"))
    resp, head = ("z", "yh", "core"), ("yl", "x")
    return jax.shard_map(
        per_device,
        mesh=fine,
        in_specs=(P(resp, head),) * 5 + (P(resp), P(head, None)),
        out_specs=P(resp, head),
        check_vma=False,
    )
```
